128 devices in a mesh: feat: 4 (over y), seed: 32 (over z, x, core).
Axes of the slice: x: 4, y: 4, z: 4, core: 2. Of those that a mesh axis runs over, the one named last changes fastest.
Arguments:
- node_feats: bfloat16 [131072, 768], P('seed', 'feat'), may hold values from -12 to 12
- seed_feats: bfloat16 [768, 32768], P('feat', 'seed'), may hold values from -6 to 6
- w_self: bfloat16 [768, 1024], P('feat'), may hold values from -0.21875 to 0.21875
- w_neigh: bfloat16 [768, 1024], P('feat'), may hold values from -0.21875 to 0.21875
- bias: float32 [1024], replicated, may hold values from -3 to 3
- send_list: int32 [32, 32, 256], P('seed'), may hold values from 0 to 4095
- nbr_slot: int32 [32768, 25], P('seed'), may hold values from 0 to 8191, as said below
- cotangent: bfloat16 [32768, 1024], P('seed', 'feat'), may hold values from -0.13183594 to 0.13183594
Outputs:
- hidden: bfloat16 [32768, 1024], P('seed', 'feat')
- grad_self: float32 [768, 1024], P('feat')
- grad_neigh: float32 [768, 1024], P('feat')
- grad_bias: float32 [1024], replicated
The draws below stay inside these ranges and needn't reach their ends.
Inputs may be any that keep to these rules, and one draw needn't show every extreme that they name: `nbr_slot`: slots may repeat; slot t names entry t % 256 of what partition t // 256 addresses to the seed's block.
All inputs are finite; a program needn't handle non-finite values.
Results may differ from the reference program's by a relative error of at most 0.003.
Values may be sent and summed in bfloat16 or wider, within the bound.
A program may use at most 448 MiB of HBM per device.

```python
import jax
import jax.numpy as jnp
from jax import lax

F = 768
H = 1024
FANOUT = 25
SEED_DEV = 1024
CAP = 256
NODE_DEV = 4096
SEEDS = 32768
NODES = 131072
N_SEED = 32


def draw_nbr_slot(key, part):
    key = jax.random.fold_in(key, 11)
    sub_keys = jax.random.split(key, 5)
    entries = SEED_DEV * FANOUT
    offset = jax.random.randint(sub_keys[0], (), 0, N_SEED)
    blocks = jnp.arange(N_SEED, dtype=jnp.int32)
    full_source = (blocks + offset) % N_SEED
    limits = jax.random.randint(sub_keys[1], (N_SEED, N_SEED), max(CAP // 4, 1), CAP + 1)
    limits = jnp.where(blocks[None, :] == full_source[:, None], CAP, limits)
    sources = jax.random.randint(sub_keys[2], (N_SEED, entries), 0, N_SEED)
    reach_top = jnp.take_along_axis(limits, sources, axis=1)
    within = jax.random.randint(sub_keys[3], (N_SEED, entries), 0, reach_top)
    marked = jax.random.randint(sub_keys[4], (N_SEED, 1), 0, entries)
    marked_spot = jnp.arange(entries, dtype=jnp.int32)[None, :] == marked
    sources = jnp.where(marked_spot, full_source[:, None], sources)
    within = jnp.where(marked_spot, CAP - 1, within)
    return (sources * CAP + within).reshape(N_SEED * SEED_DEV, FANOUT).astype(jnp.int32)


def place_ends(drawn, own_key, least, top_value):
    spot = [jax.random.randint(jax.random.fold_in(own_key, axis), (), 0, length) for axis, length in enumerate(drawn.shape)]
    widest = drawn.shape.index(max(drawn.shape))
    beside = spot[:widest] + [(spot[widest] + 1) % drawn.shape[widest]] + spot[widest + 1:]
    return drawn.at[tuple(spot)].set(least).at[tuple(beside)].set(top_value)


def shard_levels(own_key, extent, pieces, least, top_value):
    factor_of, own = 1.0, jax.random.fold_in(own_key, 6)
    for dim, shards_of in pieces:
        steps = jnp.exp(jax.random.uniform(jax.random.fold_in(own, dim), (shards_of,), jnp.float32, least / len(pieces), top_value / len(pieces)))
        factor_of = factor_of * jnp.repeat(steps, extent[dim] // shards_of).reshape([-1 if axis == dim else 1 for axis in range(len(extent))])
    return factor_of


def noise(key, extent, width, reach, pieces=(), kind=jnp.bfloat16):
    values = width * jax.random.normal(key, extent, jnp.float32)
    if pieces:
        values = values * shard_levels(key, extent, pieces, -0.22, 0.18)
    return jnp.clip(values, -reach, reach).astype(kind)


def setup_inputs(seed: int = 0) -> dict:
    seeds = jax.random.split(jax.random.key(seed), 9)
    node_feats = noise(seeds[0], (NODES, F), 2.0, 12.0, ((0, 32), (1, 4)))
    seed_feats = noise(seeds[1], (F, SEEDS), 1.0, 6.0, ((0, 4), (1, 32)))
    w_self = noise(seeds[2], (F, H), F ** -0.5, 0.21875, ((0, 4),))
    w_neigh = noise(seeds[3], (F, H), F ** -0.5, 0.21875, ((0, 4),))
    bias = noise(seeds[4], (H,), 0.5, 3.0, (), jnp.float32)
    send_list = place_ends(jax.random.randint(seeds[5], (N_SEED, N_SEED, CAP), 0, NODE_DEV), jax.random.fold_in(seeds[5], 1), 0, NODE_DEV - 1).astype(jnp.int32)
    nbr_slot = draw_nbr_slot(jax.random.fold_in(seeds[8], 71), 0)
    cotangent = noise(seeds[7], (SEEDS, H), (4.0 / (SEED_DEV * N_SEED) ** 0.5), 0.13183594, ((0, 32), (1, 4)))
    return {"node_feats": node_feats, "seed_feats": seed_feats, "w_self": w_self, "w_neigh": w_neigh, "bias": bias, "send_list": send_list, "nbr_slot": nbr_slot, "cotangent": cotangent}


def silu_slope(values):
    logistic = jax.nn.sigmoid(values)
    return logistic * (1.0 + values * (1.0 - logistic))


def reference(node_feats, seed_feats, w_self, w_neigh, bias, send_list, nbr_slot, cotangent):
    source_ids = jnp.arange(N_SEED, dtype=jnp.int32)
    node_rows = send_list + (source_ids * NODE_DEV)[:, None, None]
    slot_table = jnp.transpose(node_rows, (1, 0, 2)).reshape(N_SEED, N_SEED * CAP)
    owner_block = jnp.arange(SEEDS, dtype=jnp.int32) // SEED_DEV
    neighbour_rows = slot_table[owner_block[:, None], nbr_slot]
    summed = jnp.zeros((SEEDS, F), jnp.float32)
    for column in range(FANOUT):
        summed = summed + jnp.take(node_feats, neighbour_rows[:, column], axis=0).astype(jnp.float32)
    averaged = summed / FANOUT
    pre_whole = jnp.dot(seed_feats.T, w_self, preferred_element_type=jnp.float32)
    pre_whole = pre_whole + jnp.dot(averaged, w_neigh.astype(jnp.float32), precision=lax.Precision.HIGHEST) + bias
    hidden = jax.nn.silu(pre_whole).astype(jnp.bfloat16)
    grad_pre = (cotangent.astype(jnp.float32) * silu_slope(pre_whole)).astype(jnp.bfloat16)
    grad_self = jnp.dot(seed_feats, grad_pre, preferred_element_type=jnp.float32)
    grad_neigh = jnp.dot(averaged.T, grad_pre.astype(jnp.float32), precision=lax.Precision.HIGHEST)
    grad_bias = jnp.sum(grad_pre.astype(jnp.float32), axis=0)
    return (hidden, grad_self, grad_neigh, grad_bias)
```

```python
import jax
import jax.numpy as jnp
from jax import lax
from jax.experimental import pallas as pl
from jax.experimental.pallas import tpu as pltpu
from jax.sharding import PartitionSpec as P

MESH = pl.DeviceIdType.MESH
BF, F32, I32 = jnp.bfloat16, jnp.float32, jnp.int32
NT = (((1,), (1,)), ((), ()))


def chip_order():
    steps = []
    for a, b in ((2, 2), (1, 2), (0, 2), (1, 1), (0, 1)):
        turn = []
        for p in ((a, b), (-b, a), (-a, -b), (b, -a)):
            p = (p[0] % 4, p[1] % 4)
            if p not in turn:
                turn.append(p)
        steps += [p + (core,) for core in (0, 1) for p in turn]
    return steps


STEPS = chip_order()


def pick(values, i):
    low = sum(v << (2 * k) for k, v in enumerate(values[:15]))
    high = sum(v << (2 * k) for k, v in enumerate(values[15:]))
    return (jnp.where(i < 15, low, high) >> (2 * (i % 15))) & 3


def offset(i):
    last = i >= 30
    dz = jnp.where(last, 0, pick([s[0] for s in STEPS], i))
    dx = jnp.where(last, 0, pick([s[1] for s in STEPS], i))
    dc = jnp.where(last, 1, pick([s[2] for s in STEPS], i))
    return dz, dx, dc


def kernel(
    node, seed, w_self, w_neigh, bias, send_list, nbr, cot,
    hid, g_self, g_neigh, g_bias,
    node_t, out_rows, in_rows, counts, acc, x_self, x_a1, x_a2, wr_self, wr_a1, wr_a2,
    pre, cot_t, hid_t, gp, grad, core_in, half, red2, part2, red3, part3, full,
    bias_parts, bias_red, bias_full,
    row_send, row_recv, y_send, y_recv, d_send, d_recv,
):
    y = lax.axis_index("feat")
    me = lax.axis_index("seed")
    z, x, c = me // 8, (me // 2) % 4, me % 2

    def seed_id(z2, x2, c2):
        return (z2 * 4 + x2) * 2 + c2

    def at(feat, seed_index):
        return {"feat": feat, "seed": seed_index}

    def target(i):
        dz, dx, dc = offset(i)
        oz = jnp.where(c == 1, -dx, dz)
        ox = jnp.where(c == 1, dz, dx)
        return seed_id((z + oz + 4) % 4, (x + ox + 4) % 4, (c + dc) % 2)

    def source(i):
        dz, dx, dc = offset(i)
        c2 = (c + dc) % 2
        oz = jnp.where(c2 == 1, -dx, dz)
        ox = jnp.where(c2 == 1, dz, dx)
        return seed_id((z - oz + 4) % 4, (x - ox + 4) % 4, c2)

    barrier = pltpu.get_barrier_semaphore()

    def greet(t, _):
        pl.semaphore_signal(
            barrier, inc=1, device_id=at(y, (me + t) % 32), device_id_type=MESH
        )
        return 0

    lax.fori_loop(1, 32, greet, 0)
    for k in (1, 2, 3):
        pl.semaphore_signal(
            barrier, inc=1, device_id=at((y + k) % 4, me), device_id_type=MESH
        )

    for j in range(16):
        block = node[j * 256 : (j + 1) * 256, :].T
        for q in range(3):
            start = q * 1024 + j * 64
            node_t[start : start + 64, :] = block[q * 64 : (q + 1) * 64, :]

    pl.semaphore_wait(barrier, 34)

    def y_copy(kind, src, dst, peer):
        return pltpu.make_async_remote_copy(
            src_ref=src,
            dst_ref=dst,
            send_sem=y_send.at[kind, peer],
            recv_sem=y_recv.at[kind, y],
            device_id=at(peer, me),
            device_id_type=MESH,
        )

    def y_arrival(kind, src, dst, peer):
        return pltpu.make_async_remote_copy(
            src_ref=src,
            dst_ref=dst,
            send_sem=y_send.at[kind, peer],
            recv_sem=y_recv.at[kind, peer],
            device_id=at(peer, me),
            device_id_type=MESH,
        )

    def cols(peer):
        return pl.ds(pl.multiple_of(peer * 256, 256), 256)

    peers = [(y + k) % 4 for k in (1, 3, 2)]
    for peer in peers:
        y_copy(0, w_self.at[:, cols(peer)], wr_self.at[y], peer).start()
        y_copy(1, w_neigh.at[pl.ds(0, 128), cols(peer)], wr_a1.at[y], peer).start()
        y_copy(2, w_neigh.at[pl.ds(128, 64), cols(peer)], wr_a2.at[y], peer).start()
    for peer in peers:
        y_copy(3, seed, x_self.at[y], peer).start()
    wr_self[y] = w_self[:, cols(y)]
    wr_a1[y] = w_neigh[0:128, cols(y)]
    wr_a2[y] = w_neigh[128:192, cols(y)]
    x_self[y] = seed[...]

    def row_copy(part, to, sender):
        rows = pl.ds(0, 128) if part == 0 else pl.ds(128, 64)
        return pltpu.make_async_remote_copy(
            src_ref=out_rows.at[to, rows],
            dst_ref=in_rows.at[sender, rows],
            send_sem=row_send.at[part, to],
            recv_sem=row_recv.at[part, sender],
            device_id=at(y, to),
            device_id_type=MESH,
        )

    ids = lax.broadcasted_iota(I32, (256, 256), 0)
    in_group = lax.broadcasted_iota(I32, (1, 256), 1) // 32

    def one_hot(row):
        return jnp.where(ids == row, 1.0, 0.0).astype(BF)

    def gather_step(i, _):
        to = jnp.where(i == 31, me, target(i))
        index = send_list[pl.ds(to, 1), :]
        block, chosen = index // 256, one_hot(index % 256)
        for q in range(3):
            every = jnp.dot(
                node_t[q * 1024 : (q + 1) * 1024, :], chosen, preferred_element_type=F32
            )
            rows = jnp.zeros((64, 256), F32)
            for j in range(16):
                rows = jnp.where(block == j, every[j * 64 : (j + 1) * 64], rows)
            out_rows[to, q * 64 : (q + 1) * 64, :] = rows.astype(BF)

        @pl.when(i < 31)
        def _():
            row_copy(0, to, me).start()

        for e in range(2):
            group = 2 * i + e
            found = []
            for h in range(2):
                slot = nbr[pl.ds(2 * group + h, 1), :]
                key = jnp.where(slot < 0, -1, (slot // 256) * 8 + in_group)
                hits = lax.dot_general(
                    one_hot(key), one_hot(slot % 256), NT, preferred_element_type=F32
                )
                found.append(hits.reshape(32, 8, 256))
            counts[:, pl.ds(pl.multiple_of(group * 16, 16), 16), :] = jnp.concatenate(
                found, axis=1
            ).astype(BF)
        return 0

    lax.fori_loop(0, 32, gather_step, 0)

    def second_step(i, _):
        row_copy(1, target(i), me).start()
        return 0

    lax.fori_loop(0, 31, second_step, 0)

    def add_up(part):
        lo, n = (0, 128) if part == 0 else (128, 64)

        def term(rows, sender):
            return lax.dot_general(
                rows, counts[sender], NT, preferred_element_type=F32
            )

        def arrived(i):
            sender = source(i)
            row_copy(part, sender, sender).wait_recv()
            return term(in_rows[sender, lo : lo + n, :], sender)

        first = term(out_rows[me, lo : lo + n, :], me)
        for i in range(3):
            first = first + arrived(i)
        acc[lo : lo + n, :] = first

        def four(g, _):
            more = arrived(4 * g + 3)
            for i in range(1, 4):
                more = more + arrived(4 * g + 3 + i)
            acc[lo : lo + n, :] += more
            return 0

        lax.fori_loop(0, 7, four, 0)
        return (acc[lo : lo + n, :] * (1.0 / 25.0)).astype(BF)

    x_a1[y] = add_up(0)
    for peer in peers:
        y_copy(4, x_a1.at[y], x_a1.at[y], peer).start()

    for peer in peers:
        y_arrival(0, w_self.at[:, cols(peer)], wr_self.at[peer], peer).wait_recv()
        y_arrival(3, seed, x_self.at[peer], peer).wait_recv()
    own_bias = jnp.broadcast_to(bias[:, cols(y)], (128, 256)).T
    own_bias = jnp.concatenate([own_bias] * 8, axis=1)
    pre[...] = own_bias + jnp.dot(
        wr_self[...].reshape(768, 256).T,
        x_self[...].reshape(768, 1024),
        preferred_element_type=F32,
    )
    cot_t[...] = cot[...].T.astype(F32)

    x_a2[y] = add_up(1)
    for peer in peers:
        y_copy(5, x_a2.at[y], x_a2.at[y], peer).start()

    for peer in peers:
        y_arrival(1, w_neigh.at[pl.ds(0, 128), cols(peer)], wr_a1.at[peer], peer).wait_recv()
        y_arrival(2, w_neigh.at[pl.ds(128, 64), cols(peer)], wr_a2.at[peer], peer).wait_recv()
        y_arrival(4, x_a1.at[peer], x_a1.at[peer], peer).wait_recv()
    pre[...] += jnp.dot(
        wr_a1[...].reshape(512, 256).T,
        x_a1[...].reshape(512, 1024),
        preferred_element_type=F32,
    )
    for peer in peers:
        y_arrival(5, x_a2.at[peer], x_a2.at[peer], peer).wait_recv()
    pre[...] += jnp.dot(
        wr_a2[...].reshape(256, 256).T,
        x_a2[...].reshape(256, 1024),
        preferred_element_type=F32,
    )

    def activate(b, _):
        rows = pl.ds(pl.multiple_of(b * 32, 32), 32)
        v = pre[rows, :]
        s = 1.0 / (1.0 + jnp.exp(-v))
        hid_t[rows, :] = (v * s).astype(BF)
        gp[rows, :] = (cot_t[rows, :] * (s * (1.0 + v * (1.0 - s)))).astype(BF)
        return 0

    lax.fori_loop(0, 8, activate, 0)

    def weigh(b, _):
        for source_rows, lo, n in ((x_self, 0, 192), (x_a1, 192, 128), (x_a2, 320, 64)):
            value = lax.dot_general(
                source_rows[b], gp[...], NT, preferred_element_type=F32
            )
            rows = pl.ds(pl.multiple_of(b * 384 + lo, 64), n)
            grad[0, rows, :] = value[:, :128]
            grad[1, rows, :] = value[:, 128:]
        return 0

    lax.fori_loop(0, 4, weigh, 0)
    ones = jnp.ones((16, 1024), BF)
    bias_parts[0] = lax.dot_general(ones, gp[...], NT, preferred_element_type=F32)[:8]

    def d_copy(kind, src, dst, to_sem, from_sem, device):
        return pltpu.make_async_remote_copy(
            src_ref=src,
            dst_ref=dst,
            send_sem=d_send.at[kind, to_sem],
            recv_sem=d_recv.at[kind, from_sem],
            device_id=device,
            device_id_type=MESH,
        )

    other = at(y, seed_id(z, x, 1 - c))
    ahead = (1, 3, 2)

    def along_x(x2):
        return at(y, seed_id(z, x2, c))

    def along_z(z2):
        return at(y, seed_id(z2, x, c))

    core_copy = d_copy(0, grad.at[1 - c], core_in, 0, 0, other)
    core_bias = d_copy(1, bias_parts.at[0], bias_red.at[0], 0, 0, other)
    core_copy.start()
    core_bias.start()
    hid[...] = hid_t[...].T
    core_copy.wait_recv()
    core_bias.wait_recv()
    half[...] = (grad[c] + core_in[...]).reshape(4, 384, 128)
    bias_parts[1] = bias_parts[0] + bias_red[0]

    def piece(i, n):
        return pl.ds(pl.multiple_of(i * n, n), n)

    orders = ((x, along_x, z, along_z), (z, along_z, x, along_x))
    sent = [core_copy, core_bias]
    for k in ahead:
        for o, (mine, along, _, _) in enumerate(orders):
            to = (mine + k) % 4
            copy = d_copy(
                2 + o, half.at[pl.ds(2 * o, 2), piece(to, 96)], red2.at[o, mine], to, mine, along(to)
            )
            copy.start()
            sent.append(copy)
        to = (x + k) % 4
        copy = d_copy(4, bias_parts.at[1], bias_red.at[1 + x], to, x, along_x(to))
        copy.start()
        sent.append(copy)
    for o, (mine, along, _, _) in enumerate(orders):
        total = half[2 * o : 2 * o + 2, piece(mine, 96), :]
        for k in ahead:
            fr = (mine + k) % 4
            d_copy(
                2 + o, half.at[pl.ds(2 * o, 2), piece(fr, 96)], red2.at[o, fr], fr, fr, along(fr)
            ).wait_recv()
            total = total + red2[o, fr]
        part2[o] = total
    total = bias_parts[1]
    for k in ahead:
        fr = (x + k) % 4
        d_copy(4, bias_parts.at[1], bias_red.at[1 + fr], fr, fr, along_x(fr)).wait_recv()
        total = total + bias_red[1 + fr]
    bias_parts[2] = total

    for k in ahead:
        for o, (_, _, mine, along) in enumerate(orders):
            to = (mine + k) % 4
            copy = d_copy(
                5 + o, part2.at[o, :, piece(to, 24)], red3.at[o, mine], to, mine, along(to)
            )
            copy.start()
            sent.append(copy)
        to = (z + k) % 4
        copy = d_copy(7, bias_parts.at[2], bias_red.at[5 + z], to, z, along_z(to))
        copy.start()
        sent.append(copy)
    for o, (_, _, mine, along) in enumerate(orders):
        total = part2[o, :, piece(mine, 24), :]
        for k in ahead:
            fr = (mine + k) % 4
            d_copy(
                5 + o, part2.at[o, :, piece(fr, 24)], red3.at[o, fr], fr, fr, along(fr)
            ).wait_recv()
            total = total + red3[o, fr]
        part3[2 * o : 2 * o + 2] = total
    total = bias_parts[2]
    for k in ahead:
        fr = (z + k) % 4
        d_copy(7, bias_parts.at[2], bias_red.at[5 + fr], fr, fr, along_z(fr)).wait_recv()
        total = total + bias_red[5 + fr]
    bias_full[y] = total

    def first_axis(feat):
        return jnp.where(feat < 2, x, z)

    def second_axis(feat):
        return jnp.where(feat < 2, z, x)

    for k in ahead:
        to = (y + k) % 4
        copy = d_copy(
            8, part3.at[to], full.at[c, first_axis(to), second_axis(to), y], to, y, at(to, me)
        )
        copy.start()
        sent.append(copy)
        copy = d_copy(9, bias_full.at[y], bias_full.at[y], to, y, at(to, me))
        copy.start()
        sent.append(copy)
    i, j = first_axis(y), second_axis(y)
    full[c, i, j, y] = part3[y]
    for k in ahead:
        fr = (y + k) % 4
        d_copy(8, part3.at[fr], full.at[c, i, j, fr], fr, fr, at(fr, me)).wait_recv()
        d_copy(9, bias_full.at[fr], bias_full.at[fr], fr, fr, at(fr, me)).wait_recv()

    def along_first(i2):
        return at(y, jnp.where(y < 2, seed_id(z, i2, c), seed_id(i2, x, c)))

    def along_second(j2):
        return at(y, jnp.where(y < 2, seed_id(j2, x, c), seed_id(z, j2, c)))

    a, b = pl.ds(0, 2), pl.ds(2, 2)
    for k in ahead:
        to = (j + k) % 4
        copy = d_copy(10, full.at[c, i, j, a], full.at[c, i, j, a], to, j, along_second(to))
        copy.start()
        sent.append(copy)
        to = (i + k) % 4
        copy = d_copy(11, full.at[c, i, j, b], full.at[c, i, j, b], to, i, along_first(to))
        copy.start()
        sent.append(copy)
    for k in ahead:
        fr = (j + k) % 4
        d_copy(10, full.at[c, i, j, a], full.at[c, i, fr, a], fr, fr, along_second(fr)).wait_recv()
        fr = (i + k) % 4
        d_copy(11, full.at[c, i, j, b], full.at[c, fr, j, b], fr, fr, along_first(fr)).wait_recv()
    for k in ahead:
        to = (i + k) % 4
        copy = d_copy(12, full.at[c, i, :, a], full.at[c, i, :, a], to, i, along_first(to))
        copy.start()
        sent.append(copy)
        to = (j + k) % 4
        copy = d_copy(13, full.at[c, :, j, b], full.at[c, :, j, b], to, j, along_second(to))
        copy.start()
        sent.append(copy)
    for k in ahead:
        fr = (i + k) % 4
        d_copy(12, full.at[c, i, :, a], full.at[c, fr, :, a], fr, fr, along_first(fr)).wait_recv()
        fr = (j + k) % 4
        d_copy(13, full.at[c, :, j, b], full.at[c, :, fr, b], fr, fr, along_second(fr)).wait_recv()
    copy = d_copy(14, full.at[c], full.at[c], 0, 0, other)
    copy.start()
    sent.append(copy)
    d_copy(14, full.at[c], full.at[1 - c], 0, 0, other).wait_recv()

    for p in range(16):
        ref, row = (g_self, 24 * p) if p < 8 else (g_neigh, 24 * (p - 8))
        for q in range(8):
            ref[row : row + 24, q * 128 : (q + 1) * 128] = full[q % 2, p // 4, p % 4, q // 2]
    for q in range(4):
        g_bias[:, q * 256 : (q + 1) * 256] = bias_full[q, 0:1, :]

    for copy in sent:
        copy.wait_send()
    for peer in peers:
        y_copy(0, w_self.at[:, cols(peer)], wr_self.at[y], peer).wait_send()
        y_copy(1, w_neigh.at[pl.ds(0, 128), cols(peer)], wr_a1.at[y], peer).wait_send()
        y_copy(2, w_neigh.at[pl.ds(128, 64), cols(peer)], wr_a2.at[y], peer).wait_send()
        y_copy(3, seed, x_self.at[y], peer).wait_send()
        y_copy(4, x_a1.at[y], x_a1.at[y], peer).wait_send()
        y_copy(5, x_a2.at[y], x_a2.at[y], peer).wait_send()

    def left(i, _):
        row_copy(0, target(i), me).wait_send()
        row_copy(1, target(i), me).wait_send()
        return 0

    lax.fori_loop(0, 31, left, 0)


def local(node_feats, seed_feats, w_self, w_neigh, bias, send_list, nbr_slot, cotangent):
    nbr = jnp.pad(nbr_slot, ((0, 0), (0, 7)), constant_values=-1).reshape(128, 256)
    vmem = pl.BlockSpec(memory_space=pltpu.VMEM)
    V, DMA = pltpu.VMEM, pltpu.SemaphoreType.DMA
    hidden, grad_self, grad_neigh, grad_bias = pl.pallas_call(
        kernel,
        out_shape=(
            jax.ShapeDtypeStruct((1024, 256), BF),
            jax.ShapeDtypeStruct((192, 1024), F32),
            jax.ShapeDtypeStruct((192, 1024), F32),
            jax.ShapeDtypeStruct((1, 1024), F32),
        ),
        in_specs=[vmem] * 8,
        out_specs=(vmem,) * 4,
        scratch_shapes=[
            V((3072, 256), BF),
            V((32, 192, 256), BF),
            V((32, 192, 256), BF),
            V((32, 1024, 256), BF),
            V((192, 1024), F32),
            V((4, 192, 1024), BF),
            V((4, 128, 1024), BF),
            V((4, 64, 1024), BF),
            V((4, 192, 256), BF),
            V((4, 128, 256), BF),
            V((4, 64, 256), BF),
            V((256, 1024), F32),
            V((256, 1024), F32),
            V((256, 1024), BF),
            V((256, 1024), BF),
            V((2, 1536, 128), F32),
            V((1536, 128), F32),
            V((4, 384, 128), F32),
            V((2, 4, 2, 96, 128), F32),
            V((2, 2, 96, 128), F32),
            V((2, 4, 2, 24, 128), F32),
            V((4, 24, 128), F32),
            V((2, 4, 4, 4, 24, 128), F32),
            V((3, 8, 256), F32),
            V((9, 8, 256), F32),
            V((4, 8, 256), F32),
            DMA((2, 32)),
            DMA((2, 32)),
            DMA((6, 4)),
            DMA((6, 4)),
            DMA((15, 4)),
            DMA((15, 4)),
        ],
        compiler_params=pltpu.CompilerParams(
            collective_id=0, has_side_effects=True, vmem_limit_bytes=60 << 20
        ),
        name="sage_layer",
    )(
        node_feats,
        seed_feats,
        w_self,
        w_neigh,
        bias.reshape(1, 1024),
        send_list.reshape(32, 256),
        nbr,
        cotangent,
    )
    return hidden, grad_self, grad_neigh, grad_bias.reshape(1024)


def solution(mesh):
    placed = (
        P("seed", "feat"),
        P("feat", "seed"),
        P("feat", None),
        P("feat", None),
        P(),
        P("seed", None, None),
        P("seed", None),
        P("seed", "feat"),
    )
    return jax.shard_map(
        local,
        mesh=mesh,
        in_specs=placed,
        out_specs=(P("seed", "feat"), P("feat", None), P("feat", None), P()),
        check_vma=False,
    )
```

```python
import jax
import jax.numpy as jnp
from jax import lax
from jax.experimental import pallas as pl
from jax.experimental.pallas import tpu as pltpu
from jax.sharding import PartitionSpec as P

MESH = pl.DeviceIdType.MESH
BF, F32, I32 = jnp.bfloat16, jnp.float32, jnp.int32
NT = (((1,), (1,)), ((), ()))


def chip_order():
    steps = []
    for a, b in ((2, 2), (1, 2), (0, 2), (1, 1), (0, 1)):
        for p in ((a, b), (-b, a), (-a, -b), (b, -a)):
            p = (p[0] % 4, p[1] % 4)
            if p not in steps:
                steps.append(p)
    return steps


STEPS = chip_order()


def offset(i):
    at = 2 * (i % 16)
    dz = (sum(s[0] << (2 * k) for k, s in enumerate(STEPS)) >> at) & 3
    dx = (sum(s[1] << (2 * k) for k, s in enumerate(STEPS)) >> at) & 3
    return dz, dx, jnp.where(i >= 15, 1, 0)


def kernel(
    node, seed, w_self, w_neigh, bias, send_list, nbr, cot,
    hid, g_self, g_neigh, g_bias,
    node_t, slots, groups, out_rows, in_rows, counts, acc, x_self, x_a, wr_self, wr_a,
    pre, cot_t, hid_t, gp, grad, core_in, half, red2, part2, red3, part3, done, full,
    bias_parts, bias_red, bias_full,
    row_send, row_recv, y_send, y_recv, d_send, d_recv,
    chip_send, chip_recv, core_send, core_recv,
):
    y = lax.axis_index("feat")
    me = lax.axis_index("seed")
    z, x, c = me // 8, (me // 2) % 4, me % 2

    def seed_id(z2, x2, c2):
        return (z2 * 4 + x2) * 2 + c2

    def at(feat, seed_index):
        return {"feat": feat, "seed": seed_index}

    def target(i):
        dz, dx, dc = offset(i)
        oz = jnp.where(c == 1, -dx, dz)
        ox = jnp.where(c == 1, dz, dx)
        return seed_id((z + oz + 4) % 4, (x + ox + 4) % 4, (c + dc) % 2)

    def source(i):
        dz, dx, dc = offset(i)
        c2 = (c + dc) % 2
        oz = jnp.where(c2 == 1, -dx, dz)
        ox = jnp.where(c2 == 1, dz, dx)
        return seed_id((z - oz + 4) % 4, (x - ox + 4) % 4, c2)

    barrier = pltpu.get_barrier_semaphore()

    def greet(t, _):
        pl.semaphore_signal(
            barrier, inc=1, device_id=at(y, (me + t) % 32), device_id_type=MESH
        )
        return 0

    lax.fori_loop(1, 32, greet, 0)
    for k in (1, 2, 3):
        pl.semaphore_signal(
            barrier, inc=1, device_id=at((y + k) % 4, me), device_id_type=MESH
        )

    for j in range(16):
        for q in range(3):
            start = q * 1024 + j * 64
            node_t[start : start + 64, :] = node[
                q * 64 : (q + 1) * 64, j * 256 : (j + 1) * 256
            ]

    slots[...] = jnp.concatenate(
        [nbr[...], jnp.full((103, 1024), -1, I32)], axis=0
    ).T
    lane_group = lax.broadcasted_iota(I32, (128, 128), 1) // 32
    for part in range(2):
        line = slots[pl.ds(4 * part, 128, stride=8), :]
        for k in (1, 2, 3):
            moved = pltpu.roll(slots[pl.ds(4 * part + k, 128, stride=8), :], 32 * k, 1)
            line = jnp.where(lane_group == k, moved, line)
        groups[:, part * 128 : (part + 1) * 128] = line

    pl.semaphore_wait(barrier, 34)

    def y_copy(kind, src, dst, peer):
        return pltpu.make_async_remote_copy(
            src_ref=src,
            dst_ref=dst,
            send_sem=y_send.at[kind, peer],
            recv_sem=y_recv.at[kind, y],
            device_id=at(peer, me),
            device_id_type=MESH,
        )

    def y_arrival(kind, src, dst, peer):
        return pltpu.make_async_remote_copy(
            src_ref=src,
            dst_ref=dst,
            send_sem=y_send.at[kind, peer],
            recv_sem=y_recv.at[kind, peer],
            device_id=at(peer, me),
            device_id_type=MESH,
        )

    def cols(peer):
        return pl.ds(pl.multiple_of(peer * 256, 256), 256)

    def half_cols(peer, core):
        return pl.ds(pl.multiple_of(peer * 256 + core * 128, 128), 128)

    peers = [(y + k) % 4 for k in (1, 3, 2)]
    up, down, across = peers
    side = half_cols(0, c)
    other = at(y, seed_id(z, x, 1 - c))

    def seed_copy(peer):
        return y_copy(2, seed, x_self.at[y], peer)

    def w_copies(peer):
        own = half_cols(peer, c)
        return (
            y_copy(0, w_self.at[:, own], wr_self.at[y, :, side], peer),
            y_copy(1, w_neigh.at[:, :, own], wr_a.at[:, y, :, side], peer),
        )

    def seed_onward(way):
        fr, to, rows = (down, up, pl.ds(0, 96)) if way == 0 else (up, down, pl.ds(96, 96))
        return pltpu.make_async_remote_copy(
            src_ref=x_self.at[fr, rows],
            dst_ref=x_self.at[fr, rows],
            send_sem=y_send.at[6, way],
            recv_sem=y_recv.at[6, way],
            device_id=at(to, me),
            device_id_type=MESH,
        )

    def seed_onward_arrival(way):
        rows = pl.ds(0, 96) if way == 0 else pl.ds(96, 96)
        return pltpu.make_async_remote_copy(
            src_ref=x_self.at[across, rows],
            dst_ref=x_self.at[across, rows],
            send_sem=y_send.at[6, way],
            recv_sem=y_recv.at[6, way],
            device_id=at(up, me),
            device_id_type=MESH,
        )

    def w_to_core(kind, peer, core):
        part = half_cols(0, core)
        ref = wr_self.at[peer, :, part] if kind == 7 else wr_a.at[:, peer, :, part]
        return pltpu.make_async_remote_copy(
            src_ref=ref,
            dst_ref=ref,
            send_sem=y_send.at[kind, peer],
            recv_sem=y_recv.at[kind, peer],
            device_id=other,
            device_id_type=MESH,
        )

    for peer in (up, down):
        seed_copy(peer).start()
    for peer in peers:
        for copy in w_copies(peer):
            copy.start()
    wr_self[y] = w_self[:, cols(y)]
    for part in range(3):
        wr_a[part, y] = w_neigh[part, :, cols(y)]
    x_self[y] = seed[...]

    def row_copy(part, to, sender):
        rows = pl.ds(0, 192) if part == 3 else pl.ds(64 * part, 64)
        return pltpu.make_async_remote_copy(
            src_ref=out_rows.at[to, rows],
            dst_ref=in_rows.at[sender, rows],
            send_sem=row_send.at[part, to],
            recv_sem=row_recv.at[part, sender],
            device_id=at(y, to),
            device_id_type=MESH,
        )

    ids = lax.broadcasted_iota(I32, (256, 256), 0)
    in_group = lax.broadcasted_iota(I32, (1, 256), 1) // 32

    def one_hot(row):
        return jnp.where(ids == row, 1.0, 0.0).astype(BF)

    def gather(part, to):
        index = send_list[pl.ds(to, 1), :]
        block, chosen = index // 256, one_hot(index % 256)
        every = jnp.dot(
            node_t[part * 1024 : (part + 1) * 1024, :], chosen, preferred_element_type=F32
        )
        rows = jnp.zeros((64, 256), F32)
        for j in range(16):
            rows = jnp.where(block == j, every[j * 64 : (j + 1) * 64], rows)
        out_rows[to, part * 64 : (part + 1) * 64, :] = rows.astype(BF)

    def count(i):
        for e in range(4):
            group = 4 * i + e
            found = []
            for h in range(2):
                slot = groups[pl.ds(2 * group + h, 1), :]
                key = jnp.where(slot < 0, -1, (slot // 256) * 8 + in_group)
                hits = lax.dot_general(
                    one_hot(key), one_hot(slot % 256), NT, preferred_element_type=F32
                )
                found.append(hits.reshape(32, 8, 256))
            counts[:, pl.ds(pl.multiple_of(group * 16, 16), 16), :] = jnp.concatenate(
                found, axis=1
            ).astype(BF)

    def span(part):
        return slice(0, 192) if part == 3 else slice(64 * part, 64 * part + 64)

    def own_term(part):
        return lax.dot_general(
            out_rows[me, span(part), :], counts[me], NT, preferred_element_type=F32
        )

    def terms(part, steps):
        senders = [source(i) for i in steps]
        for sender in senders:
            row_copy(part, sender, sender).wait_recv()
        total = None
        for sender in senders:
            more = lax.dot_general(
                in_rows[sender, span(part), :], counts[sender], NT, preferred_element_type=F32
            )
            total = more if total is None else total + more
        return total

    def early_step(g, _):
        to = [target(2 * g + k) for k in range(2)]
        for k in range(2):
            for part in range(3):
                gather(part, to[k])
            count(2 * g + k)
        for k in range(2):
            row_copy(3, to[k], me).start()
        return 0

    def late_target(i):
        return jnp.where(i == 31, me, target(i))

    def late_send(part, i, to):
        @pl.when(i < 31)
        def _():
            row_copy(part, to, me).start()

    def late_first(g, _):
        steps = [16 + 4 * g + k for k in range(4)]
        to = [late_target(i) for i in steps]
        early = terms(3, [4 * g + k for k in range(4)])
        for k in range(4):
            gather(0, to[k])
        acc[...] += early
        for k in range(4):
            late_send(0, steps[k], to[k])
        return 0

    def late_rest(g, _):
        steps = [16 + 4 * g + k for k in range(4)]
        to = [late_target(i) for i in steps]
        for k in range(4):
            gather(1, to[k])
            gather(2, to[k])
        for k in range(4):
            late_send(1, steps[k], to[k])
        return 0

    def late_last(i, _):
        row_copy(2, target(i), me).start()
        return 0

    acc[...] = jnp.zeros((192, 1024), F32)
    lax.fori_loop(0, 8, early_step, 0)
    lax.fori_loop(0, 4, late_first, 0)
    for peer in (up, down):
        y_arrival(2, seed, x_self.at[peer], peer).wait_recv()
    for way in range(2):
        seed_onward(way).start()
    for peer in peers:
        own = half_cols(peer, c)
        y_arrival(0, w_self.at[:, own], wr_self.at[peer, :, side], peer).wait_recv()
        y_arrival(1, w_neigh.at[:, :, own], wr_a.at[:, peer, :, side], peer).wait_recv()
        w_to_core(7, peer, c).start()
        w_to_core(8, peer, c).start()
    lax.fori_loop(0, 4, late_rest, 0)
    lax.fori_loop(16, 31, late_last, 0)

    def add_up(part):
        rows = span(part)
        acc[rows, :] += own_term(part)

        def five(g, _):
            acc[rows, :] += terms(part, [16 + 5 * g + k for k in range(5)])
            return 0

        lax.fori_loop(0, 3, five, 0)
        x_a[part, y] = (acc[rows, :] * (1.0 / 25.0)).astype(BF)
        for peer in peers:
            y_copy(3 + part, x_a.at[part, y], x_a.at[part, y], peer).start()

    add_up(0)

    for peer in peers:
        w_to_core(7, peer, 1 - c).wait_recv()
    for way in range(2):
        seed_onward_arrival(way).wait_recv()
    own_bias = jnp.broadcast_to(bias[:, cols(y)], (128, 256)).T
    own_bias = jnp.concatenate([own_bias] * 8, axis=1)
    pre[...] = own_bias + jnp.dot(
        wr_self[...].reshape(768, 256).T,
        x_self[...].reshape(768, 1024),
        preferred_element_type=F32,
    )
    cot_t[...] = cot[...].T.astype(F32)

    add_up(1)
    add_up(2)

    for peer in peers:
        w_to_core(8, peer, 1 - c).wait_recv()
    for part in range(3):
        weight = wr_a[part].reshape(256, 256).T
        for peer in peers:
            y_arrival(3 + part, x_a.at[part, peer], x_a.at[part, peer], peer).wait_recv()
        pre[...] += jnp.dot(
            weight, x_a[part].reshape(256, 1024), preferred_element_type=F32
        )

    def activate(b, _):
        rows = pl.ds(pl.multiple_of(b * 32, 32), 32)
        v = pre[rows, :]
        s = 1.0 / (1.0 + jnp.exp(-v))
        hid_t[rows, :] = (v * s).astype(BF)
        gp[rows, :] = (cot_t[rows, :] * (s * (1.0 + v * (1.0 - s)))).astype(BF)
        return 0

    lax.fori_loop(0, 8, activate, 0)

    def weigh(b, _):
        sources = [(x_self[b], 0, 192)]
        sources += [(x_a[part, b], 192 + 64 * part, 64) for part in range(3)]
        for source_rows, lo, n in sources:
            value = lax.dot_general(source_rows, gp[...], NT, preferred_element_type=F32)
            rows = pl.ds(pl.multiple_of(b * 384 + lo, 64), n)
            grad[0, rows, :] = value[:, :128]
            grad[1, rows, :] = value[:, 128:]
        return 0

    lax.fori_loop(0, 4, weigh, 0)
    ones = jnp.ones((16, 1024), BF)
    bias_parts[0] = lax.dot_general(ones, gp[...], NT, preferred_element_type=F32)[:8]

    def d_copy(kind, src, dst, to_sem, from_sem, device):
        return pltpu.make_async_remote_copy(
            src_ref=src,
            dst_ref=dst,
            send_sem=d_send.at[kind, to_sem],
            recv_sem=d_recv.at[kind, from_sem],
            device_id=device,
            device_id_type=MESH,
        )

    ahead = (1, 3, 2)

    def along_x(x2):
        return at(y, seed_id(z, x2, c))

    def along_z(z2):
        return at(y, seed_id(z2, x, c))

    core_copy = d_copy(0, grad.at[1 - c], core_in, 0, 0, other)
    core_bias = d_copy(1, bias_parts.at[0], bias_red.at[0], 0, 0, other)
    core_copy.start()
    core_bias.start()
    hid[...] = hid_t[...].T
    core_copy.wait_recv()
    core_bias.wait_recv()
    half[...] = (grad[c] + core_in[...]).reshape(4, 384, 128)
    bias_parts[1] = bias_parts[0] + bias_red[0]

    def piece(i, n):
        return pl.ds(pl.multiple_of(i * n, n), n)

    orders = ((x, along_x, z, along_z), (z, along_z, x, along_x))
    sent = [core_copy, core_bias]
    for k in ahead:
        for o, (mine, along, _, _) in enumerate(orders):
            to = (mine + k) % 4
            copy = d_copy(
                2 + o, half.at[pl.ds(2 * o, 2), piece(to, 96)], red2.at[o, mine], to, mine, along(to)
            )
            copy.start()
            sent.append(copy)
        to = (x + k) % 4
        copy = d_copy(4, bias_parts.at[1], bias_red.at[1 + x], to, x, along_x(to))
        copy.start()
        sent.append(copy)
    for o, (mine, along, _, _) in enumerate(orders):
        total = half[2 * o : 2 * o + 2, piece(mine, 96), :]
        for k in ahead:
            fr = (mine + k) % 4
            d_copy(
                2 + o, half.at[pl.ds(2 * o, 2), piece(fr, 96)], red2.at[o, fr], fr, fr, along(fr)
            ).wait_recv()
            total = total + red2[o, fr]
        part2[o] = total
    total = bias_parts[1]
    for k in ahead:
        fr = (x + k) % 4
        d_copy(4, bias_parts.at[1], bias_red.at[1 + fr], fr, fr, along_x(fr)).wait_recv()
        total = total + bias_red[1 + fr]
    bias_parts[2] = total

    for k in ahead:
        for o, (_, _, mine, along) in enumerate(orders):
            to = (mine + k) % 4
            copy = d_copy(
                5 + o, part2.at[o, :, piece(to, 24)], red3.at[o, mine], to, mine, along(to)
            )
            copy.start()
            sent.append(copy)
        to = (z + k) % 4
        copy = d_copy(7, bias_parts.at[2], bias_red.at[5 + z], to, z, along_z(to))
        copy.start()
        sent.append(copy)
    for o, (_, _, mine, along) in enumerate(orders):
        total = part2[o, :, piece(mine, 24), :]
        for k in ahead:
            fr = (mine + k) % 4
            d_copy(
                5 + o, part2.at[o, :, piece(fr, 24)], red3.at[o, fr], fr, fr, along(fr)
            ).wait_recv()
            total = total + red3[o, fr]
        part3[2 * o : 2 * o + 2] = total
    total = bias_parts[2]
    for k in ahead:
        fr = (z + k) % 4
        d_copy(7, bias_parts.at[2], bias_red.at[5 + fr], fr, fr, along_z(fr)).wait_recv()
        total = total + bias_red[5 + fr]
    bias_full[y] = total

    for k in ahead:
        to = (y + k) % 4
        copy = d_copy(8, part3.at[to], done.at[y], to, y, at(to, me))
        copy.start()
        sent.append(copy)
        copy = d_copy(9, bias_full.at[y], bias_full.at[y], to, y, at(to, me))
        copy.start()
        sent.append(copy)
    done[y] = part3[y]
    for k in ahead:
        fr = (y + k) % 4
        d_copy(8, part3.at[fr], done.at[fr], fr, fr, at(fr, me)).wait_recv()
        d_copy(9, bias_full.at[fr], bias_full.at[fr], fr, fr, at(fr, me)).wait_recv()

    def piece_of(z2, x2):
        return jnp.where(y < 2, 4 * x2 + z2, 4 * z2 + x2)

    def turned(i):
        dz, dx, _ = offset(i)
        return jnp.where(c == 1, -dx, dz), jnp.where(c == 1, dz, dx)

    def chip_copy(i, p):
        dz, dx = turned(i)
        return pltpu.make_async_remote_copy(
            src_ref=full.at[c, p],
            dst_ref=full.at[c, p],
            send_sem=chip_send.at[i],
            recv_sem=chip_recv.at[p],
            device_id=at(y, seed_id((z + dz + 4) % 4, (x + dx + 4) % 4, c)),
            device_id_type=MESH,
        )

    def core_share(core, p):
        return pltpu.make_async_remote_copy(
            src_ref=full.at[core, p],
            dst_ref=full.at[core, p],
            send_sem=core_send.at[p],
            recv_sem=core_recv.at[p],
            device_id=other,
            device_id_type=MESH,
        )

    mine = piece_of(z, x)
    full[c, mine] = done[...].reshape(96, 128).astype(BF)

    def spread(i, _):
        chip_copy(i, mine).start()
        return 0

    lax.fori_loop(0, 15, spread, 0)
    core_share(c, mine).start()

    def collect(i, _):
        dz, dx = turned(i)
        p = piece_of((z - dz + 4) % 4, (x - dx + 4) % 4)
        chip_copy(i, p).wait_recv()
        core_share(c, p).start()
        return 0

    lax.fori_loop(0, 15, collect, 0)

    def collect_core(p, _):
        core_share(1 - c, p).wait_recv()
        return 0

    lax.fori_loop(0, 16, collect_core, 0)

    for p in range(16):
        ref, row = (g_self, 24 * p) if p < 8 else (g_neigh, 24 * (p - 8))
        for core in range(2):
            value = full[core, p].astype(F32)
            for q in range(4):
                lane = q * 256 + core * 128
                ref[row : row + 24, lane : lane + 128] = value[q * 24 : (q + 1) * 24]
    for q in range(4):
        g_bias[:, q * 256 : (q + 1) * 256] = bias_full[q, 0:1, :]

    def left_done(i, _):
        chip_copy(i, mine).wait_send()
        return 0

    lax.fori_loop(0, 15, left_done, 0)

    def left_core(p, _):
        core_share(c, p).wait_send()
        return 0

    lax.fori_loop(0, 16, left_core, 0)
    for copy in sent:
        copy.wait_send()
    for peer in peers:
        for copy in w_copies(peer):
            copy.wait_send()
        w_to_core(7, peer, c).wait_send()
        w_to_core(8, peer, c).wait_send()
        for part in range(3):
            y_copy(3 + part, x_a.at[part, y], x_a.at[part, y], peer).wait_send()

    for k in range(2):
        seed_copy((up, down)[k]).wait_send()
        seed_onward(k).wait_send()

    def left(i, _):
        for part in range(3):
            row_copy(part, target(i), me).wait_send()
        return 0

    def left_whole(i, _):
        row_copy(3, target(i), me).wait_send()
        return 0

    lax.fori_loop(16, 31, left, 0)
    lax.fori_loop(0, 16, left_whole, 0)


def hand_over(*refs):
    for made, out in zip(refs[:4], refs[4:]):
        out[...] = made[...]


def local(node_feats, seed_feats, w_self, w_neigh, bias, send_list, nbr_slot, cotangent):
    vmem = pl.BlockSpec(memory_space=pltpu.VMEM)
    V, DMA = pltpu.VMEM, pltpu.SemaphoreType.DMA
    made = pl.pallas_call(
        kernel,
        out_shape=(
            jax.ShapeDtypeStruct((1024, 256), BF),
            jax.ShapeDtypeStruct((192, 1024), F32),
            jax.ShapeDtypeStruct((192, 1024), F32),
            jax.ShapeDtypeStruct((1, 1024), F32),
        ),
        in_specs=[vmem] * 8,
        out_specs=(vmem,) * 4,
        scratch_shapes=[
            V((3072, 256), BF),
            V((1024, 128), I32),
            V((128, 256), I32),
            V((32, 192, 256), BF),
            V((32, 192, 256), BF),
            V((32, 1024, 256), BF),
            V((192, 1024), F32),
            V((4, 192, 1024), BF),
            V((3, 4, 64, 1024), BF),
            V((4, 192, 256), BF),
            V((3, 4, 64, 256), BF),
            V((256, 1024), F32),
            V((256, 1024), F32),
            V((256, 1024), BF),
            V((256, 1024), BF),
            V((2, 1536, 128), F32),
            V((1536, 128), F32),
            V((4, 384, 128), F32),
            V((2, 4, 2, 96, 128), F32),
            V((2, 2, 96, 128), F32),
            V((2, 4, 2, 24, 128), F32),
            V((4, 24, 128), F32),
            V((4, 24, 128), F32),
            V((2, 16, 96, 128), BF),
            V((3, 8, 256), F32),
            V((9, 8, 256), F32),
            V((4, 8, 256), F32),
            DMA((4, 32)),
            DMA((4, 32)),
            DMA((9, 4)),
            DMA((9, 4)),
            DMA((10, 4)),
            DMA((10, 4)),
            DMA((16,)),
            DMA((16,)),
            DMA((16,)),
            DMA((16,)),
        ],
        compiler_params=pltpu.CompilerParams(
            collective_id=0, has_side_effects=True, vmem_limit_bytes=60 << 20
        ),
        name="sage_layer",
    )(
        node_feats.T,
        seed_feats,
        w_self,
        w_neigh.reshape(3, 64, 1024),
        bias.reshape(1, 1024),
        send_list.reshape(32, 256),
        nbr_slot.T,
        cotangent,
    )
    hidden, grad_self, grad_neigh, grad_bias = pl.pallas_call(
        hand_over,
        out_shape=tuple(jax.ShapeDtypeStruct(m.shape, m.dtype) for m in made),
        in_specs=[vmem] * 4,
        out_specs=(vmem,) * 4,
        name="hand_over",
    )(*made)
    return hidden, grad_self, grad_neigh, grad_bias.reshape(1024)


def solution(mesh):
    placed = (
        P("seed", "feat"),
        P("feat", "seed"),
        P("feat", None),
        P("feat", None),
        P(),
        P("seed", None, None),
        P("seed", None),
        P("seed", "feat"),
    )
    return jax.shard_map(
        local,
        mesh=mesh,
        in_specs=placed,
        out_specs=(P("seed", "feat"), P("feat", None), P("feat", None), P()),
        check_vma=False,
    )
```

```python
import jax
import jax.numpy as jnp
from jax import lax
from jax.experimental import pallas as pl
from jax.experimental.pallas import tpu as pltpu
from jax.sharding import PartitionSpec as P

MESH = pl.DeviceIdType.MESH
BF, F32, I32 = jnp.bfloat16, jnp.float32, jnp.int32
NT = (((1,), (1,)), ((), ()))


def chip_order():
    steps = []
    for a, b in ((2, 2), (1, 2), (0, 2), (1, 1), (0, 1)):
        for p in ((a, b), (-b, a), (-a, -b), (b, -a)):
            p = (p[0] % 4, p[1] % 4)
            if p not in steps:
                steps.append(p)
    return steps


STEPS = chip_order()


def offset(i):
    at = 2 * (i % 16)
    dz = (sum(s[0] << (2 * k) for k, s in enumerate(STEPS)) >> at) & 3
    dx = (sum(s[1] << (2 * k) for k, s in enumerate(STEPS)) >> at) & 3
    return dz, dx, jnp.where(i >= 15, 1, 0)


def kernel(
    node, seed, w_self, w_neigh, bias_hbm, send_list_hbm, nbr_hbm, cot_hbm,
    hid, g_self, g_neigh, g_bias,
    node_t, send_list, nbr, bias, cot, slots, groups, out_rows, in_rows, counts, acc, x_self, x_a, wr_self, wr_a,
    pre, cot_t, hid_t, gp, grad, core_in, half, red2, part2, red3, part3, done, full,
    bias_parts, bias_red, bias_full,
    row_send, row_recv, y_send, y_recv, d_send, d_recv,
    chip_send, chip_recv, core_send, core_recv, load_sem,
):
    y = lax.axis_index("feat")
    me = lax.axis_index("seed")
    z, x, c = me // 8, (me // 2) % 4, me % 2

    def seed_id(z2, x2, c2):
        return (z2 * 4 + x2) * 2 + c2

    def at(feat, seed_index):
        return {"feat": feat, "seed": seed_index}

    def target(i):
        dz, dx, dc = offset(i)
        oz = jnp.where(c == 1, -dx, dz)
        ox = jnp.where(c == 1, dz, dx)
        return seed_id((z + oz + 4) % 4, (x + ox + 4) % 4, (c + dc) % 2)

    def source(i):
        dz, dx, dc = offset(i)
        c2 = (c + dc) % 2
        oz = jnp.where(c2 == 1, -dx, dz)
        ox = jnp.where(c2 == 1, dz, dx)
        return seed_id((z - oz + 4) % 4, (x - ox + 4) % 4, c2)

    barrier = pltpu.get_barrier_semaphore()

    def greet(t, _):
        pl.semaphore_signal(
            barrier, inc=1, device_id=at(y, (me + t) % 32), device_id_type=MESH
        )
        return 0

    lax.fori_loop(1, 32, greet, 0)
    for k in (1, 2, 3):
        pl.semaphore_signal(
            barrier, inc=1, device_id=at((y + k) % 4, me), device_id_type=MESH
        )

    def cols(peer):
        return pl.ds(pl.multiple_of(peer * 256, 256), 256)

    loads = [
        pltpu.make_async_copy(src, dst, load_sem.at[k])
        for k, (src, dst) in enumerate(
            [(send_list_hbm, send_list)]
            + [(node.at[:, pl.ds(256 * j, 256)], node_t.at[j]) for j in range(16)]
            + [
                (nbr_hbm, nbr),
                (w_self.at[:, cols(y)], wr_self.at[y]),
                (w_neigh.at[:, cols(y)], wr_a.at[y]),
                (seed, x_self.at[y]),
                (bias_hbm, bias),
                (cot_hbm, cot),
            ]
        )
    ]
    for load in loads:
        load.start()

    def y_copy(kind, src, dst, peer):
        return pltpu.make_async_remote_copy(
            src_ref=src,
            dst_ref=dst,
            send_sem=y_send.at[kind, peer],
            recv_sem=y_recv.at[kind, y],
            device_id=at(peer, me),
            device_id_type=MESH,
        )

    def y_arrival(kind, src, dst, peer):
        return pltpu.make_async_remote_copy(
            src_ref=src,
            dst_ref=dst,
            send_sem=y_send.at[kind, peer],
            recv_sem=y_recv.at[kind, peer],
            device_id=at(peer, me),
            device_id_type=MESH,
        )

    def half_cols(peer, core):
        return pl.ds(pl.multiple_of(peer * 256 + core * 128, 128), 128)

    peers = [(y + k) % 4 for k in (1, 3, 2)]
    up, down, across = peers
    side = half_cols(0, c)
    other = at(y, seed_id(z, x, 1 - c))

    def seed_copy(peer):
        return y_copy(2, seed, x_self.at[y], peer)

    def w_copies(peer):
        own = half_cols(peer, c)
        return (
            y_copy(0, w_self.at[:, own], wr_self.at[y, :, side], peer),
            y_copy(1, w_neigh.at[:, own], wr_a.at[y, :, side], peer),
        )

    def seed_onward(way):
        fr, to, rows = (down, up, pl.ds(0, 96)) if way == 0 else (up, down, pl.ds(96, 96))
        return pltpu.make_async_remote_copy(
            src_ref=x_self.at[fr, rows],
            dst_ref=x_self.at[fr, rows],
            send_sem=y_send.at[6, way],
            recv_sem=y_recv.at[6, way],
            device_id=at(to, me),
            device_id_type=MESH,
        )

    def seed_onward_arrival(way):
        rows = pl.ds(0, 96) if way == 0 else pl.ds(96, 96)
        return pltpu.make_async_remote_copy(
            src_ref=x_self.at[across, rows],
            dst_ref=x_self.at[across, rows],
            send_sem=y_send.at[6, way],
            recv_sem=y_recv.at[6, way],
            device_id=at(up, me),
            device_id_type=MESH,
        )

    def w_to_core(kind, peer, core):
        part = half_cols(0, core)
        ref = (wr_self if kind == 7 else wr_a).at[peer, :, part]
        return pltpu.make_async_remote_copy(
            src_ref=ref,
            dst_ref=ref,
            send_sem=y_send.at[kind, peer],
            recv_sem=y_recv.at[kind, peer],
            device_id=other,
            device_id_type=MESH,
        )

    def row_copy(part, to, sender):
        rows = pl.ds(0, 192) if part == 3 else pl.ds(64 * part, 64)
        return pltpu.make_async_remote_copy(
            src_ref=out_rows.at[to, rows],
            dst_ref=in_rows.at[sender, rows],
            send_sem=row_send.at[part, to],
            recv_sem=row_recv.at[part, sender],
            device_id=at(y, to),
            device_id_type=MESH,
        )

    ids = lax.broadcasted_iota(I32, (256, 256), 0)
    in_group = lax.broadcasted_iota(I32, (1, 256), 1) // 32

    def one_hot(row):
        return jnp.where(ids == row, 1.0, 0.0).astype(BF)

    def span(part):
        return slice(0, 192) if part == 3 else slice(64 * part, 64 * part + 64)

    def gather(part, to):
        index = send_list[pl.ds(to, 1), :]
        block, chosen = index // 256, one_hot(index % 256)
        every = jnp.dot(
            node_t[:, span(part), :].reshape(1024, 256), chosen, preferred_element_type=F32
        )
        rows = jnp.zeros((64, 256), F32)
        for j in range(16):
            rows = jnp.where(block == j, every[j * 64 : (j + 1) * 64], rows)
        out_rows[to, part * 64 : (part + 1) * 64, :] = rows.astype(BF)

    def count(i):
        for e in range(4):
            group = 4 * i + e
            found = []
            for h in range(2):
                slot = groups[pl.ds(2 * group + h, 1), :]
                key = jnp.where(slot < 0, -1, (slot // 256) * 8 + in_group)
                hits = lax.dot_general(
                    one_hot(key), one_hot(slot % 256), NT, preferred_element_type=F32
                )
                found.append(hits.reshape(32, 8, 256))
            counts[:, pl.ds(pl.multiple_of(group * 16, 16), 16), :] = jnp.concatenate(
                found, axis=1
            ).astype(BF)

    def own_term(part):
        return lax.dot_general(
            out_rows[me, span(part), :], counts[me], NT, preferred_element_type=F32
        )

    def terms(part, steps):
        senders = [source(i) for i in steps]
        for sender in senders:
            row_copy(part, sender, sender).wait_recv()
        total = None
        for sender in senders:
            more = lax.dot_general(
                in_rows[sender, span(part), :], counts[sender], NT, preferred_element_type=F32
            )
            total = more if total is None else total + more
        return total

    def early_step(g, _):
        to = [target(2 * g + k) for k in range(2)]
        for k in range(2):
            for part in range(3):
                gather(part, to[k])
            count(2 * g + k)
        for k in range(2):
            row_copy(3, to[k], me).start()
        return 0

    def late_target(i):
        return jnp.where(i == 31, me, target(i))

    def late_send(part, i, to):
        @pl.when(i < 31)
        def _():
            row_copy(part, to, me).start()

    def late_first(g, _):
        steps = [16 + 4 * g + k for k in range(4)]
        to = [late_target(i) for i in steps]
        early = terms(3, [4 * g + k for k in range(4)])
        for k in range(4):
            gather(0, to[k])
        acc[...] += early
        for k in range(4):
            late_send(0, steps[k], to[k])
        return 0

    def late_rest(g, _):
        steps = [16 + 4 * g + k for k in range(4)]
        to = [late_target(i) for i in steps]
        for k in range(4):
            gather(1, to[k])
            gather(2, to[k])
        for k in range(4):
            late_send(1, steps[k], to[k])
        return 0

    def late_last(i, _):
        row_copy(2, target(i), me).start()
        return 0

    for load in loads[:17]:
        load.wait()
    to = [target(k) for k in range(2)]
    for k in range(2):
        for part in range(3):
            gather(part, to[k])
    pl.semaphore_wait(barrier, 34)
    for k in range(2):
        row_copy(3, to[k], me).start()
    for peer in (up, down):
        seed_copy(peer).start()
    for peer in peers:
        for copy in w_copies(peer):
            copy.start()

    for load in loads[17:21]:
        load.wait()
    slots[...] = jnp.concatenate([nbr[...], jnp.full((103, 1024), -1, I32)], axis=0).T
    lane_group = lax.broadcasted_iota(I32, (128, 128), 1) // 32
    for part in range(2):
        line = slots[pl.ds(4 * part, 128, stride=8), :]
        for k in (1, 2, 3):
            moved = pltpu.roll(slots[pl.ds(4 * part + k, 128, stride=8), :], 32 * k, 1)
            line = jnp.where(lane_group == k, moved, line)
        groups[:, part * 128 : (part + 1) * 128] = line

    acc[...] = jnp.zeros((192, 1024), F32)
    lax.fori_loop(1, 8, early_step, 0)
    count(0)
    count(1)
    lax.fori_loop(0, 4, late_first, 0)
    for peer in (up, down):
        y_arrival(2, seed, x_self.at[peer], peer).wait_recv()
    for way in range(2):
        seed_onward(way).start()
    for peer in peers:
        own = half_cols(peer, c)
        y_arrival(0, w_self.at[:, own], wr_self.at[peer, :, side], peer).wait_recv()
        y_arrival(1, w_neigh.at[:, own], wr_a.at[peer, :, side], peer).wait_recv()
        w_to_core(7, peer, c).start()
        w_to_core(8, peer, c).start()
    lax.fori_loop(0, 4, late_rest, 0)
    lax.fori_loop(16, 31, late_last, 0)

    def averaged_copy(part, peer):
        ref = x_a.at[y, pl.ds(64 * part, 64)]
        return y_copy(3 + part, ref, ref, peer)

    def add_up(part):
        rows = span(part)
        acc[rows, :] += own_term(part)

        def five(g, _):
            acc[rows, :] += terms(part, [16 + 5 * g + k for k in range(5)])
            return 0

        lax.fori_loop(0, 3, five, 0)
        x_a[y, rows, :] = (acc[rows, :] * (1.0 / 25.0)).astype(BF)
        for peer in peers:
            averaged_copy(part, peer).start()

    add_up(0)

    for peer in peers:
        w_to_core(7, peer, 1 - c).wait_recv()
    for way in range(2):
        seed_onward_arrival(way).wait_recv()
    for load in loads[21:]:
        load.wait()
    own_bias = jnp.broadcast_to(bias[:, cols(y)], (128, 256)).T
    own_bias = jnp.concatenate([own_bias] * 8, axis=1)
    pre[...] = own_bias + jnp.dot(
        wr_self[...].reshape(768, 256).T,
        x_self[...].reshape(768, 1024),
        preferred_element_type=F32,
    )
    cot_t[...] = cot[...].T.astype(F32)

    add_up(1)
    add_up(2)

    for peer in peers:
        w_to_core(8, peer, 1 - c).wait_recv()
    for part in range(3):
        weight = wr_a[:, span(part), :].reshape(256, 256).T
        for peer in peers:
            ref = x_a.at[peer, pl.ds(64 * part, 64)]
            y_arrival(3 + part, ref, ref, peer).wait_recv()
        pre[...] += jnp.dot(
            weight, x_a[:, span(part), :].reshape(256, 1024), preferred_element_type=F32
        )

    def activate(b, _):
        rows = pl.ds(pl.multiple_of(b * 32, 32), 32)
        v = pre[rows, :]
        s = 1.0 / (1.0 + jnp.exp(-v))
        hid_t[rows, :] = (v * s).astype(BF)
        gp[rows, :] = (cot_t[rows, :] * (s * (1.0 + v * (1.0 - s)))).astype(BF)
        return 0

    lax.fori_loop(0, 8, activate, 0)

    def d_copy(kind, src, dst, to_sem, from_sem, device):
        return pltpu.make_async_remote_copy(
            src_ref=src,
            dst_ref=dst,
            send_sem=d_send.at[kind, to_sem],
            recv_sem=d_recv.at[kind, from_sem],
            device_id=device,
            device_id_type=MESH,
        )

    ahead = (1, 3, 2)

    def along_x(x2):
        return at(y, seed_id(z, x2, c))

    def along_z(z2):
        return at(y, seed_id(z2, x, c))

    def core_rows(o):
        return d_copy(
            0, grad.at[1 - c, pl.ds(768 * o, 768)], core_in.at[pl.ds(768 * o, 768)], o, o, other
        )

    core_bias = d_copy(1, bias_parts.at[0], bias_red.at[0], 0, 0, other)
    sent = [core_rows(0), core_rows(1), core_bias]
    for o in range(2):
        for first, source_rows in ((0, x_self), (192, x_a)):
            value = lax.dot_general(
                source_rows[2 * o : 2 * o + 2].reshape(384, 1024),
                gp[...],
                NT,
                preferred_element_type=F32,
            )
            for b in range(2):
                row = (2 * o + b) * 384 + first
                for core in range(2):
                    grad[core, row : row + 192, :] = value[
                        b * 192 : (b + 1) * 192, core * 128 : (core + 1) * 128
                    ]
        sent[o].start()
    ones = jnp.ones((16, 1024), BF)
    bias_parts[0] = lax.dot_general(ones, gp[...], NT, preferred_element_type=F32)[:8]
    core_bias.start()

    def piece(i, n):
        return pl.ds(pl.multiple_of(i * n, n), n)

    orders = ((x, along_x, z, along_z), (z, along_z, x, along_x))
    for o, (mine, along, _, _) in enumerate(orders):
        sent[o].wait_recv()
        rows = slice(768 * o, 768 * o + 768)
        half[2 * o : 2 * o + 2] = (grad[c, rows, :] + core_in[rows, :]).reshape(2, 384, 128)
        for k in ahead:
            to = (mine + k) % 4
            copy = d_copy(
                2 + o, half.at[pl.ds(2 * o, 2), piece(to, 96)], red2.at[o, mine], to, mine, along(to)
            )
            copy.start()
            sent.append(copy)
    core_bias.wait_recv()
    bias_parts[1] = bias_parts[0] + bias_red[0]
    for k in ahead:
        to = (x + k) % 4
        copy = d_copy(4, bias_parts.at[1], bias_red.at[1 + x], to, x, along_x(to))
        copy.start()
        sent.append(copy)
    hid[...] = hid_t[...].T
    for o, (mine, along, _, _) in enumerate(orders):
        total = half[2 * o : 2 * o + 2, piece(mine, 96), :]
        for k in ahead:
            fr = (mine + k) % 4
            d_copy(
                2 + o, half.at[pl.ds(2 * o, 2), piece(fr, 96)], red2.at[o, fr], fr, fr, along(fr)
            ).wait_recv()
            total = total + red2[o, fr]
        part2[o] = total
    total = bias_parts[1]
    for k in ahead:
        fr = (x + k) % 4
        d_copy(4, bias_parts.at[1], bias_red.at[1 + fr], fr, fr, along_x(fr)).wait_recv()
        total = total + bias_red[1 + fr]
    bias_parts[2] = total

    for k in ahead:
        for o, (_, _, mine, along) in enumerate(orders):
            to = (mine + k) % 4
            copy = d_copy(
                5 + o, part2.at[o, :, piece(to, 24)], red3.at[o, mine], to, mine, along(to)
            )
            copy.start()
            sent.append(copy)
        to = (z + k) % 4
        copy = d_copy(7, bias_parts.at[2], bias_red.at[5 + z], to, z, along_z(to))
        copy.start()
        sent.append(copy)
    for o, (_, _, mine, along) in enumerate(orders):
        total = part2[o, :, piece(mine, 24), :]
        for k in ahead:
            fr = (mine + k) % 4
            d_copy(
                5 + o, part2.at[o, :, piece(fr, 24)], red3.at[o, fr], fr, fr, along(fr)
            ).wait_recv()
            total = total + red3[o, fr]
        part3[2 * o : 2 * o + 2] = total
    total = bias_parts[2]
    for k in ahead:
        fr = (z + k) % 4
        d_copy(7, bias_parts.at[2], bias_red.at[5 + fr], fr, fr, along_z(fr)).wait_recv()
        total = total + bias_red[5 + fr]
    bias_full[y] = total

    for k in ahead:
        to = (y + k) % 4
        copy = d_copy(8, part3.at[to], done.at[y], to, y, at(to, me))
        copy.start()
        sent.append(copy)
        copy = d_copy(9, bias_full.at[y], bias_full.at[y], to, y, at(to, me))
        copy.start()
        sent.append(copy)
    done[y] = part3[y]
    for k in ahead:
        fr = (y + k) % 4
        d_copy(8, part3.at[fr], done.at[fr], fr, fr, at(fr, me)).wait_recv()
        d_copy(9, bias_full.at[fr], bias_full.at[fr], fr, fr, at(fr, me)).wait_recv()

    def piece_of(z2, x2):
        return jnp.where(y < 2, 4 * x2 + z2, 4 * z2 + x2)

    def turned(i):
        dz, dx, _ = offset(i)
        return jnp.where(c == 1, -dx, dz), jnp.where(c == 1, dz, dx)

    def chip_copy(i, p):
        dz, dx = turned(i)
        return pltpu.make_async_remote_copy(
            src_ref=full.at[c, p],
            dst_ref=full.at[c, p],
            send_sem=chip_send.at[i],
            recv_sem=chip_recv.at[p],
            device_id=at(y, seed_id((z + dz + 4) % 4, (x + dx + 4) % 4, c)),
            device_id_type=MESH,
        )

    def core_share(core, p):
        return pltpu.make_async_remote_copy(
            src_ref=full.at[core, p],
            dst_ref=full.at[core, p],
            send_sem=core_send.at[p],
            recv_sem=core_recv.at[p],
            device_id=other,
            device_id_type=MESH,
        )

    mine = piece_of(z, x)
    full[c, mine] = done[...].reshape(96, 128).astype(BF)

    def spread(i, _):
        chip_copy(i, mine).start()
        return 0

    lax.fori_loop(0, 15, spread, 0)
    core_share(c, mine).start()

    def collect(i, _):
        dz, dx = turned(i)
        p = piece_of((z - dz + 4) % 4, (x - dx + 4) % 4)
        chip_copy(i, p).wait_recv()
        core_share(c, p).start()
        return 0

    lax.fori_loop(0, 15, collect, 0)

    def collect_core(p, _):
        core_share(1 - c, p).wait_recv()
        return 0

    lax.fori_loop(0, 16, collect_core, 0)

    for p in range(16):
        ref, row = (g_self, 24 * p) if p < 8 else (g_neigh, 24 * (p - 8))
        for core in range(2):
            value = full[core, p].astype(F32)
            for q in range(4):
                lane = q * 256 + core * 128
                ref[row : row + 24, lane : lane + 128] = value[q * 24 : (q + 1) * 24]
    for q in range(4):
        g_bias[:, q * 256 : (q + 1) * 256] = bias_full[q, 0:1, :]

    def left_done(i, _):
        chip_copy(i, mine).wait_send()
        return 0

    lax.fori_loop(0, 15, left_done, 0)

    def left_core(p, _):
        core_share(c, p).wait_send()
        return 0

    lax.fori_loop(0, 16, left_core, 0)
    for copy in sent:
        copy.wait_send()
    for peer in peers:
        for copy in w_copies(peer):
            copy.wait_send()
        w_to_core(7, peer, c).wait_send()
        w_to_core(8, peer, c).wait_send()
        for part in range(3):
            averaged_copy(part, peer).wait_send()

    for k in range(2):
        seed_copy((up, down)[k]).wait_send()
        seed_onward(k).wait_send()

    def left(i, _):
        for part in range(3):
            row_copy(part, target(i), me).wait_send()
        return 0

    def left_whole(i, _):
        row_copy(3, target(i), me).wait_send()
        return 0

    lax.fori_loop(16, 31, left, 0)
    lax.fori_loop(0, 16, left_whole, 0)


def hand_over(*refs):
    sem_in, sem_out = refs[12:]
    inward, outward = [], []
    for made, out, held, parts in zip(refs[:4], refs[4:8], refs[8:12], (2, 2, 2, 1)):
        rows = made.shape[0] // parts
        for part in range(parts):
            k, span = len(inward), pl.ds(part * rows, rows)
            inward.append(pltpu.make_async_copy(made.at[span], held.at[span], sem_in.at[k]))
            outward.append(pltpu.make_async_copy(held.at[span], out.at[span], sem_out.at[k]))
    for copy in inward:
        copy.start()
    for there, back in zip(inward, outward):
        there.wait()
        back.start()
    for copy in outward:
        copy.wait()


def local(node_feats, seed_feats, w_self, w_neigh, bias, send_list, nbr_slot, cotangent):
    vmem = pl.BlockSpec(memory_space=pltpu.VMEM)
    V, DMA = pltpu.VMEM, pltpu.SemaphoreType.DMA
    made = pl.pallas_call(
        kernel,
        out_shape=(
            jax.ShapeDtypeStruct((1024, 256), BF),
            jax.ShapeDtypeStruct((192, 1024), F32),
            jax.ShapeDtypeStruct((192, 1024), F32),
            jax.ShapeDtypeStruct((1, 1024), F32),
        ),
        in_specs=[pl.BlockSpec(memory_space=pl.ANY)] * 8,
        out_specs=(vmem,) * 4,
        scratch_shapes=[
            V((16, 192, 256), BF),
            V((32, 256), I32),
            V((25, 1024), I32),
            V((1, 1024), F32),
            V((1024, 256), BF),
            V((1024, 128), I32),
            V((128, 256), I32),
            V((32, 192, 256), BF),
            V((32, 192, 256), BF),
            V((32, 1024, 256), BF),
            V((192, 1024), F32),
            V((4, 192, 1024), BF),
            V((4, 192, 1024), BF),
            V((4, 192, 256), BF),
            V((4, 192, 256), BF),
            V((256, 1024), F32),
            V((256, 1024), F32),
            V((256, 1024), BF),
            V((256, 1024), BF),
            V((2, 1536, 128), F32),
            V((1536, 128), F32),
            V((4, 384, 128), F32),
            V((2, 4, 2, 96, 128), F32),
            V((2, 2, 96, 128), F32),
            V((2, 4, 2, 24, 128), F32),
            V((4, 24, 128), F32),
            V((4, 24, 128), F32),
            V((2, 16, 96, 128), BF),
            V((3, 8, 256), F32),
            V((9, 8, 256), F32),
            V((4, 8, 256), F32),
            DMA((4, 32)),
            DMA((4, 32)),
            DMA((9, 4)),
            DMA((9, 4)),
            DMA((10, 4)),
            DMA((10, 4)),
            DMA((16,)),
            DMA((16,)),
            DMA((16,)),
            DMA((16,)),
            DMA((23,)),
        ],
        compiler_params=pltpu.CompilerParams(
            collective_id=0, has_side_effects=True, vmem_limit_bytes=60 << 20
        ),
        name="sage_layer",
    )(
        node_feats.T,
        seed_feats,
        w_self,
        w_neigh,
        bias.reshape(1, 1024),
        send_list.reshape(32, 256),
        nbr_slot.T,
        cotangent,
    )
    hidden, grad_self, grad_neigh, grad_bias = pl.pallas_call(
        hand_over,
        out_shape=tuple(jax.ShapeDtypeStruct(m.shape, m.dtype) for m in made),
        in_specs=[pl.BlockSpec(memory_space=pl.ANY)] * 4,
        out_specs=(pl.BlockSpec(memory_space=pl.ANY),) * 4,
        scratch_shapes=[V(m.shape, m.dtype) for m in made] + [DMA((7,)), DMA((7,))],
        name="hand_over",
    )(*made)
    return hidden, grad_self, grad_neigh, grad_bias.reshape(1024)


def solution(mesh):
    placed = (
        P("seed", "feat"),
        P("feat", "seed"),
        P("feat", None),
        P("feat", None),
        P(),
        P("seed", None, None),
        P("seed", None),
        P("seed", "feat"),
    )
    return jax.shard_map(
        local,
        mesh=mesh,
        in_specs=placed,
        out_specs=(P("seed", "feat"), P("feat", None), P("feat", None), P()),
        check_vma=False,
    )
```

```python
import jax
import jax.numpy as jnp
from jax import lax
from jax.experimental import pallas as pl
from jax.experimental.pallas import tpu as pltpu
from jax.sharding import PartitionSpec as P

MESH = pl.DeviceIdType.MESH
BF, F32, I32 = jnp.bfloat16, jnp.float32, jnp.int32
NT = (((1,), (1,)), ((), ()))


def chip_order():
    steps = []
    for a, b in ((2, 2), (1, 2), (0, 2), (1, 1), (0, 1)):
        for p in ((a, b), (-b, a), (-a, -b), (b, -a)):
            p = (p[0] % 4, p[1] % 4)
            if p not in steps:
                steps.append(p)
    return steps


STEPS = chip_order()


def offset(i):
    at = 2 * (i % 16)
    dz = (sum(s[0] << (2 * k) for k, s in enumerate(STEPS)) >> at) & 3
    dx = (sum(s[1] << (2 * k) for k, s in enumerate(STEPS)) >> at) & 3
    return dz, dx, jnp.where(i >= 15, 1, 0)


def kernel(
    node, seed, w_self, w_neigh, bias_hbm, send_list_hbm, nbr_hbm, cot_hbm,
    hid_hbm, full_hbm, g_bias,
    node_t, send_list, nbr, bias, cot, slots, groups, out_rows, in_rows, counts, acc, x_self, x_a, wr_self, wr_a,
    pre, cot_t, hid_t, hid, gp, grad, core_in, half, red2, part2, red3, full,
    bias_parts, bias_red, bias_full,
    row_send, row_recv, y_send, y_recv, d_send, d_recv,
    chip_send, chip_recv, core_send, core_recv, load_sem, out_sem, keep_send, keep_recv,
):
    y = lax.axis_index("feat")
    me = lax.axis_index("seed")
    z, x, c = me // 8, (me // 2) % 4, me % 2

    def seed_id(z2, x2, c2):
        return (z2 * 4 + x2) * 2 + c2

    def at(feat, seed_index):
        return {"feat": feat, "seed": seed_index}

    def target(i):
        dz, dx, dc = offset(i)
        oz = jnp.where(c == 1, -dx, dz)
        ox = jnp.where(c == 1, dz, dx)
        return seed_id((z + oz + 4) % 4, (x + ox + 4) % 4, (c + dc) % 2)

    def source(i):
        dz, dx, dc = offset(i)
        c2 = (c + dc) % 2
        oz = jnp.where(c2 == 1, -dx, dz)
        ox = jnp.where(c2 == 1, dz, dx)
        return seed_id((z - oz + 4) % 4, (x - ox + 4) % 4, c2)

    barrier = pltpu.get_barrier_semaphore()

    def greet(t, _):
        pl.semaphore_signal(
            barrier, inc=1, device_id=at(y, (me + t) % 32), device_id_type=MESH
        )
        return 0

    lax.fori_loop(1, 32, greet, 0)
    for k in (1, 2, 3):
        pl.semaphore_signal(
            barrier, inc=1, device_id=at((y + k) % 4, me), device_id_type=MESH
        )
        for turn in (1, 2, 3):
            for seed_index in (seed_id((z + turn) % 4, x, c), seed_id(z, (x + turn) % 4, c)):
                pl.semaphore_signal(
                    barrier, inc=1, device_id=at((y + k) % 4, seed_index), device_id_type=MESH
                )

    def cols(peer):
        return pl.ds(pl.multiple_of(peer * 256, 256), 256)

    loads = [
        pltpu.make_async_copy(src, dst, load_sem.at[k])
        for k, (src, dst) in enumerate(
            [(send_list_hbm, send_list)]
            + [(node.at[:, pl.ds(256 * j, 256)], node_t.at[j]) for j in range(16)]
            + [
                (nbr_hbm, nbr),
                (w_self.at[:, cols(y)], wr_self.at[y]),
                (w_neigh.at[:, cols(y)], wr_a.at[y]),
                (seed, x_self.at[y]),
                (bias_hbm, bias),
                (cot_hbm, cot),
            ]
        )
    ]
    for load in loads:
        load.start()

    def y_copy(kind, src, dst, peer):
        return pltpu.make_async_remote_copy(
            src_ref=src,
            dst_ref=dst,
            send_sem=y_send.at[kind, peer],
            recv_sem=y_recv.at[kind, y],
            device_id=at(peer, me),
            device_id_type=MESH,
        )

    def y_arrival(kind, src, dst, peer):
        return pltpu.make_async_remote_copy(
            src_ref=src,
            dst_ref=dst,
            send_sem=y_send.at[kind, peer],
            recv_sem=y_recv.at[kind, peer],
            device_id=at(peer, me),
            device_id_type=MESH,
        )

    def half_cols(peer, core):
        return pl.ds(pl.multiple_of(peer * 256 + core * 128, 128), 128)

    peers = [(y + k) % 4 for k in (1, 3, 2)]
    up, down, across = peers
    side = half_cols(0, c)
    other = at(y, seed_id(z, x, 1 - c))

    def seed_copy(peer):
        return y_copy(2, seed, x_self.at[y], peer)

    def w_copies(peer):
        own = half_cols(peer, c)
        return (
            y_copy(0, w_self.at[:, own], wr_self.at[y, :, side], peer),
            y_copy(1, w_neigh.at[:, own], wr_a.at[y, :, side], peer),
        )

    def seed_onward(way):
        fr, to, rows = (down, up, pl.ds(0, 96)) if way == 0 else (up, down, pl.ds(96, 96))
        return pltpu.make_async_remote_copy(
            src_ref=x_self.at[fr, rows],
            dst_ref=x_self.at[fr, rows],
            send_sem=y_send.at[6, way],
            recv_sem=y_recv.at[6, way],
            device_id=at(to, me),
            device_id_type=MESH,
        )

    def seed_onward_arrival(way):
        rows = pl.ds(0, 96) if way == 0 else pl.ds(96, 96)
        return pltpu.make_async_remote_copy(
            src_ref=x_self.at[across, rows],
            dst_ref=x_self.at[across, rows],
            send_sem=y_send.at[6, way],
            recv_sem=y_recv.at[6, way],
            device_id=at(up, me),
            device_id_type=MESH,
        )

    def w_to_core(kind, peer, core):
        part = half_cols(0, core)
        ref = (wr_self if kind == 7 else wr_a).at[peer, :, part]
        return pltpu.make_async_remote_copy(
            src_ref=ref,
            dst_ref=ref,
            send_sem=y_send.at[kind, peer],
            recv_sem=y_recv.at[kind, peer],
            device_id=other,
            device_id_type=MESH,
        )

    def row_copy(part, to, sender):
        rows = pl.ds(0, 192) if part == 3 else pl.ds(64 * part, 64)
        return pltpu.make_async_remote_copy(
            src_ref=out_rows.at[to, rows],
            dst_ref=in_rows.at[sender, rows],
            send_sem=row_send.at[part, to],
            recv_sem=row_recv.at[part, sender],
            device_id=at(y, to),
            device_id_type=MESH,
        )

    ids = lax.broadcasted_iota(I32, (256, 256), 0)
    in_group = lax.broadcasted_iota(I32, (1, 256), 1) // 32

    def one_hot(row):
        return jnp.where(ids == row, 1.0, 0.0).astype(BF)

    def span(part):
        return slice(0, 192) if part == 3 else slice(64 * part, 64 * part + 64)

    def gather(part, to):
        index = send_list[pl.ds(to, 1), :]
        block, chosen = index // 256, one_hot(index % 256)
        every = jnp.dot(
            node_t[:, span(part), :].reshape(1024, 256), chosen, preferred_element_type=F32
        )
        rows = jnp.zeros((64, 256), F32)
        for j in range(16):
            rows = jnp.where(block == j, every[j * 64 : (j + 1) * 64], rows)
        out_rows[to, part * 64 : (part + 1) * 64, :] = rows.astype(BF)

    def count(i):
        for e in range(4):
            group = 4 * i + e
            found = []
            for h in range(2):
                slot = groups[pl.ds(2 * group + h, 1), :]
                key = jnp.where(slot < 0, -1, (slot // 256) * 8 + in_group)
                hits = lax.dot_general(
                    one_hot(key), one_hot(slot % 256), NT, preferred_element_type=F32
                )
                found.append(hits.reshape(32, 8, 256))
            counts[:, pl.ds(pl.multiple_of(group * 16, 16), 16), :] = jnp.concatenate(
                found, axis=1
            ).astype(BF)

    def own_term(part):
        return lax.dot_general(
            out_rows[me, span(part), :], counts[me], NT, preferred_element_type=F32
        )

    def terms(part, steps):
        senders = [source(i) for i in steps]
        for sender in senders:
            row_copy(part, sender, sender).wait_recv()
        total = None
        for sender in senders:
            more = lax.dot_general(
                in_rows[sender, span(part), :], counts[sender], NT, preferred_element_type=F32
            )
            total = more if total is None else total + more
        return total

    def early_step(g, _):
        to = [target(2 * g + k) for k in range(2)]
        for k in range(2):
            for part in range(3):
                gather(part, to[k])
            count(2 * g + k)
        for k in range(2):
            row_copy(3, to[k], me).start()
        return 0

    def late_target(i):
        return jnp.where(i == 31, me, target(i))

    def late_send(part, i, to):
        @pl.when(i < 31)
        def _():
            row_copy(part, to, me).start()

    def late_first(g, _):
        steps = [16 + 4 * g + k for k in range(4)]
        to = [late_target(i) for i in steps]
        early = terms(3, [4 * g + k for k in range(4)])
        for k in range(4):
            gather(0, to[k])
        acc[...] += early
        for k in range(4):
            late_send(0, steps[k], to[k])
        return 0

    def late_rest(g, _):
        steps = [16 + 4 * g + k for k in range(4)]
        to = [late_target(i) for i in steps]
        for k in range(4):
            gather(1, to[k])
            gather(2, to[k])
        for k in range(4):
            late_send(1, steps[k], to[k])
        return 0

    def late_last(i, _):
        row_copy(2, target(i), me).start()
        return 0

    for load in loads[:17]:
        load.wait()
    to = [target(k) for k in range(2)]
    for k in range(2):
        for part in range(3):
            gather(part, to[k])
    pl.semaphore_wait(barrier, 52)
    for k in range(2):
        row_copy(3, to[k], me).start()
    for peer in (up, down):
        seed_copy(peer).start()
    for peer in peers:
        for copy in w_copies(peer):
            copy.start()

    for load in loads[17:21]:
        load.wait()
    slots[...] = jnp.concatenate([nbr[...], jnp.full((103, 1024), -1, I32)], axis=0).T
    lane_group = lax.broadcasted_iota(I32, (128, 128), 1) // 32
    for part in range(2):
        line = slots[pl.ds(4 * part, 128, stride=8), :]
        for k in (1, 2, 3):
            moved = pltpu.roll(slots[pl.ds(4 * part + k, 128, stride=8), :], 32 * k, 1)
            line = jnp.where(lane_group == k, moved, line)
        groups[:, part * 128 : (part + 1) * 128] = line

    acc[...] = jnp.zeros((192, 1024), F32)
    lax.fori_loop(1, 8, early_step, 0)
    count(0)
    count(1)
    lax.fori_loop(0, 4, late_first, 0)
    for peer in (up, down):
        y_arrival(2, seed, x_self.at[peer], peer).wait_recv()
    for way in range(2):
        seed_onward(way).start()
    for peer in peers:
        own = half_cols(peer, c)
        y_arrival(0, w_self.at[:, own], wr_self.at[peer, :, side], peer).wait_recv()
        y_arrival(1, w_neigh.at[:, own], wr_a.at[peer, :, side], peer).wait_recv()
        w_to_core(7, peer, c).start()
        w_to_core(8, peer, c).start()
    lax.fori_loop(0, 4, late_rest, 0)
    lax.fori_loop(16, 31, late_last, 0)

    def averaged_ref(part, owner):
        if part < 2:
            return x_a.at[owner, pl.ds(64 * part, 64)]
        return x_a.at[owner, pl.ds(128, 64), pl.ds(512 * (part - 2), 512)]

    def averaged_copy(part, peer):
        ref = averaged_ref(part, y)
        return y_copy((3, 4, 5, 9)[part], ref, ref, peer)

    def averaged_arrival(part, peer):
        ref = averaged_ref(part, peer)
        return y_arrival((3, 4, 5, 9)[part], ref, ref, peer)

    def add_up(part):
        rows = span(part)
        acc[rows, :] += own_term(part)

        def five(g, _):
            acc[rows, :] += terms(part, [16 + 5 * g + k for k in range(5)])
            return 0

        lax.fori_loop(0, 3, five, 0)
        x_a[y, rows, :] = (acc[rows, :] * (1.0 / 25.0)).astype(BF)
        for piece in (part,) if part < 2 else (2, 3):
            for peer in peers:
                averaged_copy(piece, peer).start()

    add_up(0)

    for peer in peers:
        w_to_core(7, peer, 1 - c).wait_recv()
    for way in range(2):
        seed_onward_arrival(way).wait_recv()
    for load in loads[21:]:
        load.wait()
    own_bias = jnp.broadcast_to(bias[:, cols(y)], (128, 256)).T
    own_bias = jnp.concatenate([own_bias] * 8, axis=1)
    pre[...] = own_bias + jnp.dot(
        wr_self[...].reshape(768, 256).T,
        x_self[...].reshape(768, 1024),
        preferred_element_type=F32,
    )
    cot_t[...] = cot[...].T.astype(F32)

    add_up(1)
    add_up(2)

    for peer in peers:
        w_to_core(8, peer, 1 - c).wait_recv()
    for part in range(2):
        weight = wr_a[:, span(part), :].reshape(256, 256).T
        for peer in peers:
            averaged_arrival(part, peer).wait_recv()
        pre[...] += jnp.dot(
            weight, x_a[:, span(part), :].reshape(256, 1024), preferred_element_type=F32
        )

    weight = wr_a[:, span(2), :].reshape(256, 256).T
    for h in range(2):
        lanes = slice(512 * h, 512 * h + 512)
        for peer in peers:
            averaged_arrival(2 + h, peer).wait_recv()
        pre[:, lanes] += jnp.dot(
            weight, x_a[:, span(2), lanes].reshape(256, 512), preferred_element_type=F32
        )

        def activate(b, _):
            rows = pl.ds(pl.multiple_of(b * 64, 64), 64)
            v = pre[rows, lanes]
            s = 1.0 / (1.0 + jnp.exp(-v))
            hid_t[rows, lanes] = (v * s).astype(BF)
            gp[rows, lanes] = (cot_t[rows, lanes] * (s * (1.0 + v * (1.0 - s)))).astype(BF)
            return 0

        lax.fori_loop(0, 4, activate, 0)

    def d_copy(kind, src, dst, to_sem, from_sem, device):
        return pltpu.make_async_remote_copy(
            src_ref=src,
            dst_ref=dst,
            send_sem=d_send.at[kind, to_sem],
            recv_sem=d_recv.at[kind, from_sem],
            device_id=device,
            device_id_type=MESH,
        )

    ahead = (1, 3, 2)

    def along_x(x2):
        return at(y, seed_id(z, x2, c))

    def along_z(z2):
        return at(y, seed_id(z2, x, c))

    def core_rows(o):
        return d_copy(
            0, grad.at[1 - c, pl.ds(768 * o, 768)], core_in.at[pl.ds(768 * o, 768)], o, o, other
        )

    core_bias = d_copy(1, bias_parts.at[0], bias_red.at[0], 0, 0, other)
    sent = [core_rows(0), core_rows(1), core_bias]
    for o in range(2):
        for first, source_rows in ((0, x_self), (192, x_a)):
            value = lax.dot_general(
                source_rows[2 * o : 2 * o + 2].reshape(384, 1024),
                gp[...],
                NT,
                preferred_element_type=F32,
            )
            for b in range(2):
                row = (2 * o + b) * 384 + first
                for core in range(2):
                    grad[core, row : row + 192, :] = value[
                        b * 192 : (b + 1) * 192, core * 128 : (core + 1) * 128
                    ]
        sent[o].start()
    ones = jnp.ones((16, 1024), BF)
    bias_parts[0] = lax.dot_general(ones, gp[...], NT, preferred_element_type=F32)[:8]
    core_bias.start()

    def piece(i, n):
        return pl.ds(pl.multiple_of(i * n, n), n)

    orders = ((x, along_x, z, along_z), (z, along_z, x, along_x))
    for o, (mine, along, _, _) in enumerate(orders):
        sent[o].wait_recv()
        rows = slice(768 * o, 768 * o + 768)
        half[2 * o : 2 * o + 2] = (grad[c, rows, :] + core_in[rows, :]).reshape(2, 384, 128)
        for k in ahead:
            to = (mine + k) % 4
            copy = d_copy(
                2 + o, half.at[pl.ds(2 * o, 2), piece(to, 96)], red2.at[o, mine], to, mine, along(to)
            )
            copy.start()
            sent.append(copy)
    core_bias.wait_recv()
    bias_parts[1] = bias_parts[0] + bias_red[0]
    for k in ahead:
        to = (x + k) % 4
        copy = d_copy(4, bias_parts.at[1], bias_red.at[1 + x], to, x, along_x(to))
        copy.start()
        sent.append(copy)
    hid[...] = hid_t[...].T
    hid_out = pltpu.make_async_copy(hid, hid_hbm, out_sem.at[32])
    hid_out.start()

    for peer in peers:
        for copy in w_copies(peer):
            copy.wait_send()
        w_to_core(7, peer, c).wait_send()
        w_to_core(8, peer, c).wait_send()
        for part in range(4):
            averaged_copy(part, peer).wait_send()

    for k in range(2):
        seed_copy((up, down)[k]).wait_send()
        seed_onward(k).wait_send()

    def left(i, _):
        for part in range(3):
            row_copy(part, target(i), me).wait_send()
        return 0

    def left_whole(i, _):
        row_copy(3, target(i), me).wait_send()
        return 0

    lax.fori_loop(16, 31, left, 0)
    lax.fori_loop(0, 16, left_whole, 0)

    for o, (mine, along, _, _) in enumerate(orders):
        total = half[2 * o : 2 * o + 2, piece(mine, 96), :]
        for k in ahead:
            fr = (mine + k) % 4
            d_copy(
                2 + o, half.at[pl.ds(2 * o, 2), piece(fr, 96)], red2.at[o, fr], fr, fr, along(fr)
            ).wait_recv()
            total = total + red2[o, fr]
        part2[o] = total
    total = bias_parts[1]
    for k in ahead:
        fr = (x + k) % 4
        d_copy(4, bias_parts.at[1], bias_red.at[1 + fr], fr, fr, along_x(fr)).wait_recv()
        total = total + bias_red[1 + fr]
    bias_parts[2] = total

    def keep(o, r, k):
        mine = orders[o][2]
        j = (mine + k) % 4
        feat = 2 * o + r
        return pltpu.make_async_remote_copy(
            src_ref=part2.at[o, r, piece(j, 24)],
            dst_ref=red3.at[y, mine],
            send_sem=keep_send.at[feat, j],
            recv_sem=keep_recv.at[y, mine],
            device_id=at(feat, seed_id(j, x, c) if o == 0 else seed_id(z, j, c)),
            device_id_type=MESH,
        )

    def each_kept(act):
        for k in (2, 1, 3, 0):
            for r in range(2):
                for o in range(2):
                    if k:
                        act(keep(o, r, k))
                    else:

                        @pl.when(y != 2 * o + r)
                        def _():
                            act(keep(o, r, 0))

    each_kept(lambda copy: copy.start())
    for k in ahead:
        to = (z + k) % 4
        copy = d_copy(7, bias_parts.at[2], bias_red.at[5 + z], to, z, along_z(to))
        copy.start()
        sent.append(copy)
    j0 = jnp.where(y < 2, z, x)
    red3[y, j0] = part2[y // 2, y % 2, piece(j0, 24), :]
    for ky in range(4):
        for kj in range(4):
            if ky or kj:
                fr_y, fr_j = (y + ky) % 4, (j0 + kj) % 4
                pltpu.make_async_remote_copy(
                    src_ref=red3.at[fr_y, fr_j],
                    dst_ref=red3.at[fr_y, fr_j],
                    send_sem=keep_send.at[fr_y, fr_j],
                    recv_sem=keep_recv.at[fr_y, fr_j],
                    device_id=other,
                    device_id_type=MESH,
                ).wait_recv()
    done = red3[:, 0] + red3[:, 1] + red3[:, 2] + red3[:, 3]

    def piece_of(z2, x2):
        return jnp.where(y < 2, 4 * x2 + z2, 4 * z2 + x2)

    def turned(i):
        dz, dx, _ = offset(i)
        return jnp.where(c == 1, -dx, dz), jnp.where(c == 1, dz, dx)

    def chip_copy(i, p):
        dz, dx = turned(i)
        return pltpu.make_async_remote_copy(
            src_ref=full.at[c, p],
            dst_ref=full.at[c, p],
            send_sem=chip_send.at[i],
            recv_sem=chip_recv.at[p],
            device_id=at(y, seed_id((z + dz + 4) % 4, (x + dx + 4) % 4, c)),
            device_id_type=MESH,
        )

    def core_share(core, p):
        return pltpu.make_async_remote_copy(
            src_ref=full.at[core, p],
            dst_ref=full.at[core, p],
            send_sem=core_send.at[p],
            recv_sem=core_recv.at[p],
            device_id=other,
            device_id_type=MESH,
        )

    def piece_out(core, p):
        return pltpu.make_async_copy(
            full.at[core, p], full_hbm.at[core, p], out_sem.at[16 * core + p]
        )

    mine = piece_of(z, x)
    full[c, mine] = done.reshape(96, 128).astype(BF)

    for i in range(15):
        chip_copy(i, mine).start()
    core_share(c, mine).start()
    piece_out(c, mine).start()

    total = bias_parts[2]
    for k in ahead:
        fr = (z + k) % 4
        d_copy(7, bias_parts.at[2], bias_red.at[5 + fr], fr, fr, along_z(fr)).wait_recv()
        total = total + bias_red[5 + fr]
    bias_full[y] = total
    for k in ahead:
        to = (y + k) % 4
        copy = d_copy(9, bias_full.at[y], bias_full.at[y], to, y, at(to, me))
        copy.start()
        sent.append(copy)

    def collect(i, _):
        dz, dx = turned(i)
        p = piece_of((z - dz + 4) % 4, (x - dx + 4) % 4)
        chip_copy(i, p).wait_recv()
        core_share(c, p).start()
        piece_out(c, p).start()
        return 0

    lax.fori_loop(0, 15, collect, 0)

    def collect_core(p, _):
        core_share(1 - c, p).wait_recv()
        piece_out(1 - c, p).start()
        return 0

    lax.fori_loop(0, 16, collect_core, 0)

    for k in ahead:
        fr = (y + k) % 4
        d_copy(9, bias_full.at[fr], bias_full.at[fr], fr, fr, at(fr, me)).wait_recv()
    for q in range(4):
        g_bias[:, q * 256 : (q + 1) * 256] = bias_full[q, 0:1, :]

    def left_done(i, _):
        chip_copy(i, mine).wait_send()
        return 0

    lax.fori_loop(0, 15, left_done, 0)

    def left_core(p, _):
        core_share(c, p).wait_send()
        piece_out(0, p).wait()
        piece_out(1, p).wait()
        return 0

    lax.fori_loop(0, 16, left_core, 0)
    each_kept(lambda copy: copy.wait_send())
    hid_out.wait()
    for copy in sent:
        copy.wait_send()


def hand_over(
    hid_in, pieces_in, bias_in, hid, g_self, g_neigh, g_bias,
    hid_held, pieces, grads, bias_held, sem_in, sem_out,
):
    def quarter(i):
        return pl.ds(4 * i, 4)

    halves = [pl.ds(512 * h, 512) for h in range(2)]
    inward = [
        pltpu.make_async_copy(pieces_in.at[:, quarter(i)], pieces.at[:, quarter(i)], sem_in.at[i])
        for i in range(4)
    ]
    inward += [
        pltpu.make_async_copy(hid_in.at[h], hid_held.at[h], sem_in.at[4 + k])
        for k, h in enumerate(halves)
    ]
    inward += [pltpu.make_async_copy(bias_in, bias_held, sem_in.at[6])]
    outward = [
        pltpu.make_async_copy(
            grads.at[pl.ds(96 * i, 96)],
            (g_self, g_neigh)[i // 2].at[pl.ds(96 * (i % 2), 96)],
            sem_out.at[i],
        )
        for i in range(4)
    ]
    outward += [
        pltpu.make_async_copy(hid_held.at[h], hid.at[h], sem_out.at[4 + k])
        for k, h in enumerate(halves)
    ]
    outward += [pltpu.make_async_copy(bias_held, g_bias, sem_out.at[6])]
    for copy in inward:
        copy.start()
    for i in (0, 1, 2, 3, 4, 5, 6):
        inward[i].wait()
        if i < 4:
            for p in range(4 * i, 4 * i + 4):
                for core in range(2):
                    value = pieces[core, p].astype(F32)
                    for q in range(4):
                        lane = q * 256 + core * 128
                        grads[24 * p : 24 * p + 24, lane : lane + 128] = value[
                            24 * q : 24 * q + 24
                        ]
        outward[i].start()
    for copy in outward:
        copy.wait()


def local(node_feats, seed_feats, w_self, w_neigh, bias, send_list, nbr_slot, cotangent):
    vmem = pl.BlockSpec(memory_space=pltpu.VMEM)
    anywhere = pl.BlockSpec(memory_space=pl.ANY)
    V, DMA = pltpu.VMEM, pltpu.SemaphoreType.DMA
    made = pl.pallas_call(
        kernel,
        out_shape=(
            jax.ShapeDtypeStruct((1024, 256), BF),
            jax.ShapeDtypeStruct((2, 16, 96, 128), BF),
            jax.ShapeDtypeStruct((1, 1024), F32),
        ),
        in_specs=[anywhere] * 8,
        out_specs=(anywhere, anywhere, vmem),
        scratch_shapes=[
            V((16, 192, 256), BF),
            V((32, 256), I32),
            V((25, 1024), I32),
            V((1, 1024), F32),
            V((1024, 256), BF),
            V((1024, 128), I32),
            V((128, 256), I32),
            V((32, 192, 256), BF),
            V((32, 192, 256), BF),
            V((32, 1024, 256), BF),
            V((192, 1024), F32),
            V((4, 192, 1024), BF),
            V((4, 192, 1024), BF),
            V((4, 192, 256), BF),
            V((4, 192, 256), BF),
            V((256, 1024), F32),
            V((256, 1024), F32),
            V((256, 1024), BF),
            V((1024, 256), BF),
            V((256, 1024), BF),
            V((2, 1536, 128), F32),
            V((1536, 128), F32),
            V((4, 384, 128), F32),
            V((2, 4, 2, 96, 128), F32),
            V((2, 2, 96, 128), F32),
            V((4, 4, 24, 128), F32),
            V((2, 16, 96, 128), BF),
            V((3, 8, 256), F32),
            V((9, 8, 256), F32),
            V((4, 8, 256), F32),
            DMA((4, 32)),
            DMA((4, 32)),
            DMA((10, 4)),
            DMA((10, 4)),
            DMA((10, 4)),
            DMA((10, 4)),
            DMA((16,)),
            DMA((16,)),
            DMA((16,)),
            DMA((16,)),
            DMA((23,)),
            DMA((33,)),
            DMA((4, 4)),
            DMA((4, 4)),
        ],
        compiler_params=pltpu.CompilerParams(
            collective_id=0, has_side_effects=True, vmem_limit_bytes=60 << 20
        ),
        name="sage_layer",
    )(
        node_feats.T,
        seed_feats,
        w_self,
        w_neigh,
        bias.reshape(1, 1024),
        send_list.reshape(32, 256),
        nbr_slot.T,
        cotangent,
    )
    hidden, grad_self, grad_neigh, grad_bias = pl.pallas_call(
        hand_over,
        out_shape=(
            jax.ShapeDtypeStruct((1024, 256), BF),
            jax.ShapeDtypeStruct((192, 1024), F32),
            jax.ShapeDtypeStruct((192, 1024), F32),
            jax.ShapeDtypeStruct((1, 1024), F32),
        ),
        in_specs=[anywhere] * 3,
        out_specs=(anywhere,) * 4,
        scratch_shapes=[
            V((1024, 256), BF),
            V((2, 16, 96, 128), BF),
            V((384, 1024), F32),
            V((1, 1024), F32),
            DMA((7,)),
            DMA((7,)),
        ],
        name="hand_over",
    )(*made)
    return hidden, grad_self, grad_neigh, grad_bias.reshape(1024)


def solution(mesh):
    placed = (
        P("seed", "feat"),
        P("feat", "seed"),
        P("feat", None),
        P("feat", None),
        P(),
        P("seed", None, None),
        P("seed", None),
        P("seed", "feat"),
    )
    return jax.shard_map(
        local,
        mesh=mesh,
        in_specs=placed,
        out_specs=(P("seed", "feat"), P("feat", None), P("feat", None), P()),
        check_vma=False,
    )
```

```python
import jax
import jax.numpy as jnp
from jax import lax
from jax.experimental import pallas as pl
from jax.experimental.pallas import tpu as pltpu
from jax.sharding import PartitionSpec as P

MESH = pl.DeviceIdType.MESH
BF, F32, I32 = jnp.bfloat16, jnp.float32, jnp.int32
NT = (((1,), (1,)), ((), ()))


def chip_order():
    steps = []
    for a, b in ((2, 2), (1, 2), (0, 2), (1, 1), (0, 1)):
        for p in ((a, b), (-b, a), (-a, -b), (b, -a)):
            p = (p[0] % 4, p[1] % 4)
            if p not in steps:
                steps.append(p)
    return steps


STEPS = chip_order()


def offset(i):
    at = 2 * (i % 16)
    dz = (sum(s[0] << (2 * k) for k, s in enumerate(STEPS)) >> at) & 3
    dx = (sum(s[1] << (2 * k) for k, s in enumerate(STEPS)) >> at) & 3
    return dz, dx, jnp.where(i >= 15, 1, 0)


def kernel(
    node, seed, w_self, w_neigh, bias_hbm, send_list_hbm, nbr_hbm, cot_hbm,
    hid_hbm, full_hbm, g_bias,
    node_t, send_list, nbr, bias, cot, slots, groups, out_rows, in_rows, counts, acc, x_self, x_a, wr_self, wr_a,
    pre, cot_t, hid_t, hid, gp, grad, core_in, half, red2, part2, red3, full,
    bias_parts, bias_red, bias_full,
    row_send, row_recv, y_send, y_recv, d_send, d_recv,
    chip_send, chip_recv, core_send, core_recv, load_sem, out_sem, keep_send, keep_recv,
):
    y = lax.axis_index("feat")
    me = lax.axis_index("seed")
    z, x, c = me // 8, (me // 2) % 4, me % 2

    def seed_id(z2, x2, c2):
        return (z2 * 4 + x2) * 2 + c2

    def at(feat, seed_index):
        return {"feat": feat, "seed": seed_index}

    def target(i):
        dz, dx, dc = offset(i)
        oz = jnp.where(c == 1, -dx, dz)
        ox = jnp.where(c == 1, dz, dx)
        return seed_id((z + oz + 4) % 4, (x + ox + 4) % 4, (c + dc) % 2)

    def source(i):
        dz, dx, dc = offset(i)
        c2 = (c + dc) % 2
        oz = jnp.where(c2 == 1, -dx, dz)
        ox = jnp.where(c2 == 1, dz, dx)
        return seed_id((z - oz + 4) % 4, (x - ox + 4) % 4, c2)

    barrier = pltpu.get_barrier_semaphore()

    def greet(t, _):
        pl.semaphore_signal(
            barrier, inc=1, device_id=at(y, (me + t) % 32), device_id_type=MESH
        )
        return 0

    lax.fori_loop(1, 32, greet, 0)
    for k in (1, 2, 3):
        pl.semaphore_signal(
            barrier, inc=1, device_id=at((y + k) % 4, me), device_id_type=MESH
        )
        for turn in (1, 2, 3):
            for seed_index in (seed_id((z + turn) % 4, x, c), seed_id(z, (x + turn) % 4, c)):
                pl.semaphore_signal(
                    barrier, inc=1, device_id=at((y + k) % 4, seed_index), device_id_type=MESH
                )

    def cols(peer):
        return pl.ds(pl.multiple_of(peer * 256, 256), 256)

    loads = [
        pltpu.make_async_copy(src, dst, load_sem.at[k])
        for k, (src, dst) in enumerate(
            [(send_list_hbm, send_list)]
            + [(node.at[:, pl.ds(256 * j, 256)], node_t.at[j]) for j in range(16)]
            + [
                (nbr_hbm, nbr),
                (w_self.at[:, cols(y)], wr_self.at[y]),
                (w_neigh.at[:, cols(y)], wr_a.at[y]),
                (seed, x_self.at[y]),
                (bias_hbm, bias),
                (cot_hbm, cot),
            ]
        )
    ]
    for load in loads:
        load.start()

    def y_copy(kind, src, dst, peer):
        return pltpu.make_async_remote_copy(
            src_ref=src,
            dst_ref=dst,
            send_sem=y_send.at[kind, peer],
            recv_sem=y_recv.at[kind, y],
            device_id=at(peer, me),
            device_id_type=MESH,
        )

    def y_arrival(kind, src, dst, peer):
        return pltpu.make_async_remote_copy(
            src_ref=src,
            dst_ref=dst,
            send_sem=y_send.at[kind, peer],
            recv_sem=y_recv.at[kind, peer],
            device_id=at(peer, me),
            device_id_type=MESH,
        )

    def half_cols(peer, core):
        return pl.ds(pl.multiple_of(peer * 256 + core * 128, 128), 128)

    peers = [(y + k) % 4 for k in (1, 3, 2)]
    up, down, across = peers
    side = half_cols(0, c)
    other = at(y, seed_id(z, x, 1 - c))

    def seed_copy(peer):
        return y_copy(2, seed, x_self.at[y], peer)

    def w_copies(peer):
        own = half_cols(peer, c)
        return (
            y_copy(0, w_self.at[:, own], wr_self.at[y, :, side], peer),
            y_copy(1, w_neigh.at[:, own], wr_a.at[y, :, side], peer),
        )

    def seed_onward(way):
        fr, to, rows = (down, up, pl.ds(0, 96)) if way == 0 else (up, down, pl.ds(96, 96))
        return pltpu.make_async_remote_copy(
            src_ref=x_self.at[fr, rows],
            dst_ref=x_self.at[fr, rows],
            send_sem=y_send.at[6, way],
            recv_sem=y_recv.at[6, way],
            device_id=at(to, me),
            device_id_type=MESH,
        )

    def seed_onward_arrival(way):
        rows = pl.ds(0, 96) if way == 0 else pl.ds(96, 96)
        return pltpu.make_async_remote_copy(
            src_ref=x_self.at[across, rows],
            dst_ref=x_self.at[across, rows],
            send_sem=y_send.at[6, way],
            recv_sem=y_recv.at[6, way],
            device_id=at(up, me),
            device_id_type=MESH,
        )

    def w_to_core(kind, peer, core):
        part = half_cols(0, core)
        ref = (wr_self if kind == 7 else wr_a).at[peer, :, part]
        return pltpu.make_async_remote_copy(
            src_ref=ref,
            dst_ref=ref,
            send_sem=y_send.at[kind, peer],
            recv_sem=y_recv.at[kind, peer],
            device_id=other,
            device_id_type=MESH,
        )

    def row_copy(part, to, sender):
        rows = pl.ds(0, 192) if part == 3 else pl.ds(64 * part, 64)
        return pltpu.make_async_remote_copy(
            src_ref=out_rows.at[to, rows],
            dst_ref=in_rows.at[sender, rows],
            send_sem=row_send.at[part, to],
            recv_sem=row_recv.at[part, sender],
            device_id=at(y, to),
            device_id_type=MESH,
        )

    ids = lax.broadcasted_iota(I32, (256, 256), 0)
    in_group = lax.broadcasted_iota(I32, (1, 256), 1) // 32

    def one_hot(row):
        return jnp.where(ids == row, 1.0, 0.0).astype(BF)

    def span(part):
        return slice(0, 192) if part == 3 else slice(64 * part, 64 * part + 64)

    def gather(part, to):
        index = send_list[pl.ds(to, 1), :]
        block, chosen = index // 256, one_hot(index % 256)
        every = jnp.dot(
            node_t[:, span(part), :].reshape(1024, 256), chosen, preferred_element_type=F32
        )
        rows = jnp.zeros((64, 256), F32)
        for j in range(16):
            rows = jnp.where(block == j, every[j * 64 : (j + 1) * 64], rows)
        out_rows[to, part * 64 : (part + 1) * 64, :] = rows.astype(BF)

    def count(i):
        for e in range(4):
            group = 4 * i + e
            found = []
            for h in range(2):
                slot = groups[pl.ds(2 * group + h, 1), :]
                key = jnp.where(slot < 0, -1, (slot // 256) * 8 + in_group)
                hits = lax.dot_general(
                    one_hot(key), one_hot(slot % 256), NT, preferred_element_type=F32
                )
                found.append(hits.reshape(32, 8, 256))
            counts[:, pl.ds(pl.multiple_of(group * 16, 16), 16), :] = jnp.concatenate(
                found, axis=1
            ).astype(BF)

    def own_term(part):
        return lax.dot_general(
            out_rows[me, span(part), :], counts[me], NT, preferred_element_type=F32
        )

    def terms(part, steps):
        senders = [source(i) for i in steps]
        for sender in senders:
            row_copy(part, sender, sender).wait_recv()
        total = None
        for sender in senders:
            more = lax.dot_general(
                in_rows[sender, span(part), :], counts[sender], NT, preferred_element_type=F32
            )
            total = more if total is None else total + more
        return total

    def early_step(g, _):
        to = [target(2 * g + k) for k in range(2)]
        for k in range(2):
            for part in range(3):
                gather(part, to[k])
            count(2 * g + k)
        for k in range(2):
            row_copy(3, to[k], me).start()
        return 0

    def late_target(i):
        return jnp.where(i == 31, me, target(i))

    def late_send(part, i, to):
        @pl.when(i < 31)
        def _():
            row_copy(part, to, me).start()

    def late_first(g, _):
        steps = [16 + 4 * g + k for k in range(4)]
        to = [late_target(i) for i in steps]
        early = terms(3, [4 * g + k for k in range(4)])
        for k in range(4):
            gather(0, to[k])
        acc[...] += early
        for k in range(4):
            late_send(0, steps[k], to[k])
        return 0

    def late_rest(g, _):
        steps = [16 + 4 * g + k for k in range(4)]
        to = [late_target(i) for i in steps]
        for k in range(4):
            gather(1, to[k])
            gather(2, to[k])
        for k in range(4):
            late_send(1, steps[k], to[k])
        return 0

    def late_last(i, _):
        row_copy(2, target(i), me).start()
        return 0

    for load in loads[:17]:
        load.wait()
    to = [target(k) for k in range(2)]
    for k in range(2):
        for part in range(3):
            gather(part, to[k])
    pl.semaphore_wait(barrier, 52)
    for k in range(2):
        row_copy(3, to[k], me).start()
    for peer in (up, down):
        seed_copy(peer).start()
    for peer in peers:
        for copy in w_copies(peer):
            copy.start()

    for load in loads[17:21]:
        load.wait()
    slots[...] = jnp.concatenate([nbr[...], jnp.full((103, 1024), -1, I32)], axis=0).T
    lane_group = lax.broadcasted_iota(I32, (128, 128), 1) // 32
    for part in range(2):
        line = slots[pl.ds(4 * part, 128, stride=8), :]
        for k in (1, 2, 3):
            moved = pltpu.roll(slots[pl.ds(4 * part + k, 128, stride=8), :], 32 * k, 1)
            line = jnp.where(lane_group == k, moved, line)
        groups[:, part * 128 : (part + 1) * 128] = line

    acc[...] = jnp.zeros((192, 1024), F32)
    lax.fori_loop(1, 8, early_step, 0)
    count(0)
    count(1)
    lax.fori_loop(0, 4, late_first, 0)
    for peer in (up, down):
        y_arrival(2, seed, x_self.at[peer], peer).wait_recv()
    for way in range(2):
        seed_onward(way).start()
    for peer in peers:
        own = half_cols(peer, c)
        y_arrival(0, w_self.at[:, own], wr_self.at[peer, :, side], peer).wait_recv()
        y_arrival(1, w_neigh.at[:, own], wr_a.at[peer, :, side], peer).wait_recv()
        w_to_core(7, peer, c).start()
        w_to_core(8, peer, c).start()
    lax.fori_loop(0, 4, late_rest, 0)
    lax.fori_loop(16, 31, late_last, 0)

    def averaged_ref(part, owner):
        if part < 2:
            return x_a.at[owner, pl.ds(64 * part, 64)]
        return x_a.at[owner, pl.ds(128, 64), pl.ds(512 * (part - 2), 512)]

    def averaged_copy(part, peer):
        ref = averaged_ref(part, y)
        return y_copy((3, 4, 5, 9)[part], ref, ref, peer)

    def averaged_arrival(part, peer):
        ref = averaged_ref(part, peer)
        return y_arrival((3, 4, 5, 9)[part], ref, ref, peer)

    def add_up(part):
        rows = span(part)
        acc[rows, :] += own_term(part)

        def five(g, _):
            acc[rows, :] += terms(part, [16 + 5 * g + k for k in range(5)])
            return 0

        lax.fori_loop(0, 3, five, 0)
        x_a[y, rows, :] = (acc[rows, :] * (1.0 / 25.0)).astype(BF)
        for piece in (part,) if part < 2 else (2, 3):
            for peer in (across, up, down):
                averaged_copy(piece, peer).start()

    add_up(0)

    for peer in peers:
        w_to_core(7, peer, 1 - c).wait_recv()
    for way in range(2):
        seed_onward_arrival(way).wait_recv()
    for load in loads[21:]:
        load.wait()
    own_bias = jnp.broadcast_to(bias[:, cols(y)], (128, 256)).T
    own_bias = jnp.concatenate([own_bias] * 8, axis=1)
    pre[...] = own_bias + jnp.dot(
        wr_self[...].reshape(768, 256).T,
        x_self[...].reshape(768, 1024),
        preferred_element_type=F32,
    )
    cot_t[...] = cot[...].T.astype(F32)

    add_up(1)
    add_up(2)

    for peer in peers:
        w_to_core(8, peer, 1 - c).wait_recv()
    for part in range(2):
        weight = wr_a[:, span(part), :].reshape(256, 256).T
        for peer in peers:
            averaged_arrival(part, peer).wait_recv()
        pre[...] += jnp.dot(
            weight, x_a[:, span(part), :].reshape(256, 1024), preferred_element_type=F32
        )

    weight = wr_a[:, span(2), :].reshape(256, 256).T
    for h in range(2):
        lanes = slice(512 * h, 512 * h + 512)
        for peer in peers:
            averaged_arrival(2 + h, peer).wait_recv()
        pre[:, lanes] += jnp.dot(
            weight, x_a[:, span(2), lanes].reshape(256, 512), preferred_element_type=F32
        )

        def activate(b, _):
            rows = pl.ds(pl.multiple_of(b * 64, 64), 64)
            v = pre[rows, lanes]
            s = 1.0 / (1.0 + jnp.exp(-v))
            hid_t[rows, lanes] = (v * s).astype(BF)
            gp[rows, lanes] = (cot_t[rows, lanes] * (s * (1.0 + v * (1.0 - s)))).astype(BF)
            return 0

        lax.fori_loop(0, 4, activate, 0)

    def d_copy(kind, src, dst, to_sem, from_sem, device):
        return pltpu.make_async_remote_copy(
            src_ref=src,
            dst_ref=dst,
            send_sem=d_send.at[kind, to_sem],
            recv_sem=d_recv.at[kind, from_sem],
            device_id=device,
            device_id_type=MESH,
        )

    ahead = (2, 1, 3)

    def along_x(x2):
        return at(y, seed_id(z, x2, c))

    def along_z(z2):
        return at(y, seed_id(z2, x, c))

    def core_rows(o):
        return d_copy(
            0, grad.at[1 - c, pl.ds(768 * o, 768)], core_in.at[pl.ds(768 * o, 768)], o, o, other
        )

    core_bias = d_copy(1, bias_parts.at[0], bias_red.at[0], 0, 0, other)
    sent = [core_rows(0), core_rows(1), core_bias]
    for o in range(2):
        for first, source_rows in ((0, x_self), (192, x_a)):
            value = lax.dot_general(
                source_rows[2 * o : 2 * o + 2].reshape(384, 1024),
                gp[...],
                NT,
                preferred_element_type=F32,
            )
            for b in range(2):
                row = (2 * o + b) * 384 + first
                for core in range(2):
                    grad[core, row : row + 192, :] = value[
                        b * 192 : (b + 1) * 192, core * 128 : (core + 1) * 128
                    ]
        sent[o].start()
    ones = jnp.ones((16, 1024), BF)
    bias_parts[0] = lax.dot_general(ones, gp[...], NT, preferred_element_type=F32)[:8]
    core_bias.start()

    def piece(i, n):
        return pl.ds(pl.multiple_of(i * n, n), n)

    orders = ((x, along_x, z, along_z), (z, along_z, x, along_x))
    for o, (mine, along, _, _) in enumerate(orders):
        sent[o].wait_recv()
        rows = slice(768 * o, 768 * o + 768)
        half[2 * o : 2 * o + 2] = (grad[c, rows, :] + core_in[rows, :]).reshape(2, 384, 128)
        for k in ahead:
            to = (mine + k) % 4
            copy = d_copy(
                2 + o, half.at[pl.ds(2 * o, 2), piece(to, 96)], red2.at[o, mine], to, mine, along(to)
            )
            copy.start()
            sent.append(copy)
    core_bias.wait_recv()
    bias_parts[1] = bias_parts[0] + bias_red[0]
    for k in ahead:
        to = (x + k) % 4
        copy = d_copy(4, bias_parts.at[1], bias_red.at[1 + x], to, x, along_x(to))
        copy.start()
        sent.append(copy)
    hid[...] = hid_t[...].T
    hid_out = pltpu.make_async_copy(hid, hid_hbm, out_sem.at[32])
    hid_out.start()

    for peer in peers:
        for copy in w_copies(peer):
            copy.wait_send()
        w_to_core(7, peer, c).wait_send()
        w_to_core(8, peer, c).wait_send()
        for part in range(4):
            averaged_copy(part, peer).wait_send()

    for k in range(2):
        seed_copy((up, down)[k]).wait_send()
        seed_onward(k).wait_send()

    def left(i, _):
        for part in range(3):
            row_copy(part, target(i), me).wait_send()
        return 0

    def left_whole(i, _):
        row_copy(3, target(i), me).wait_send()
        return 0

    lax.fori_loop(16, 31, left, 0)
    lax.fori_loop(0, 16, left_whole, 0)

    for o, (mine, along, _, _) in enumerate(orders):
        total = half[2 * o : 2 * o + 2, piece(mine, 96), :]
        for k in ahead:
            fr = (mine + k) % 4
            d_copy(
                2 + o, half.at[pl.ds(2 * o, 2), piece(fr, 96)], red2.at[o, fr], fr, fr, along(fr)
            ).wait_recv()
            total = total + red2[o, fr]
        part2[o] = total
    total = bias_parts[1]
    for k in ahead:
        fr = (x + k) % 4
        d_copy(4, bias_parts.at[1], bias_red.at[1 + fr], fr, fr, along_x(fr)).wait_recv()
        total = total + bias_red[1 + fr]
    bias_parts[2] = total

    def keep(o, r, k):
        mine = orders[o][2]
        j = (mine + k) % 4
        feat = 2 * o + r
        return pltpu.make_async_remote_copy(
            src_ref=part2.at[o, r, piece(j, 24)],
            dst_ref=red3.at[y, mine],
            send_sem=keep_send.at[feat, j],
            recv_sem=keep_recv.at[y, mine],
            device_id=at(feat, seed_id(j, x, c) if o == 0 else seed_id(z, j, c)),
            device_id_type=MESH,
        )

    def each_kept(act):
        for k in (2, 1, 3, 0):
            for r in range(2):
                for o in range(2):
                    if k:
                        act(keep(o, r, k))
                    else:

                        @pl.when(y != 2 * o + r)
                        def _():
                            act(keep(o, r, 0))

    each_kept(lambda copy: copy.start())
    for k in ahead:
        to = (z + k) % 4
        copy = d_copy(7, bias_parts.at[2], bias_red.at[5 + z], to, z, along_z(to))
        copy.start()
        sent.append(copy)
    j0 = jnp.where(y < 2, z, x)
    red3[y, j0] = part2[y // 2, y % 2, piece(j0, 24), :]
    for ky in range(4):
        for kj in range(4):
            if ky or kj:
                fr_y, fr_j = (y + ky) % 4, (j0 + kj) % 4
                pltpu.make_async_remote_copy(
                    src_ref=red3.at[fr_y, fr_j],
                    dst_ref=red3.at[fr_y, fr_j],
                    send_sem=keep_send.at[fr_y, fr_j],
                    recv_sem=keep_recv.at[fr_y, fr_j],
                    device_id=other,
                    device_id_type=MESH,
                ).wait_recv()
    done = red3[:, 0] + red3[:, 1] + red3[:, 2] + red3[:, 3]

    def piece_of(z2, x2):
        return jnp.where(y < 2, 4 * x2 + z2, 4 * z2 + x2)

    def turned(i):
        dz, dx, _ = offset(i)
        return jnp.where(c == 1, -dx, dz), jnp.where(c == 1, dz, dx)

    def chip_copy(i, p):
        dz, dx = turned(i)
        return pltpu.make_async_remote_copy(
            src_ref=full.at[c, p],
            dst_ref=full.at[c, p],
            send_sem=chip_send.at[i],
            recv_sem=chip_recv.at[p],
            device_id=at(y, seed_id((z + dz + 4) % 4, (x + dx + 4) % 4, c)),
            device_id_type=MESH,
        )

    def core_share(core, p):
        return pltpu.make_async_remote_copy(
            src_ref=full.at[core, p],
            dst_ref=full.at[core, p],
            send_sem=core_send.at[p],
            recv_sem=core_recv.at[p],
            device_id=other,
            device_id_type=MESH,
        )

    def piece_out(core, p):
        return pltpu.make_async_copy(
            full.at[core, p], full_hbm.at[core, p], out_sem.at[16 * core + p]
        )

    mine = piece_of(z, x)
    full[c, mine] = done.reshape(96, 128).astype(BF)

    for i in range(15):
        chip_copy(i, mine).start()
    core_share(c, mine).start()
    piece_out(c, mine).start()

    total = bias_parts[2]
    for k in ahead:
        fr = (z + k) % 4
        d_copy(7, bias_parts.at[2], bias_red.at[5 + fr], fr, fr, along_z(fr)).wait_recv()
        total = total + bias_red[5 + fr]
    bias_full[y] = total
    for k in ahead:
        to = (y + k) % 4
        copy = d_copy(9, bias_full.at[y], bias_full.at[y], to, y, at(to, me))
        copy.start()
        sent.append(copy)

    def collect(i, _):
        dz, dx = turned(i)
        p = piece_of((z - dz + 4) % 4, (x - dx + 4) % 4)
        chip_copy(i, p).wait_recv()
        core_share(c, p).start()
        piece_out(c, p).start()
        return 0

    lax.fori_loop(0, 15, collect, 0)

    def collect_core(p, _):
        core_share(1 - c, p).wait_recv()
        piece_out(1 - c, p).start()
        return 0

    lax.fori_loop(0, 16, collect_core, 0)

    for k in ahead:
        fr = (y + k) % 4
        d_copy(9, bias_full.at[fr], bias_full.at[fr], fr, fr, at(fr, me)).wait_recv()
    for q in range(4):
        g_bias[:, q * 256 : (q + 1) * 256] = bias_full[q, 0:1, :]

    def left_done(i, _):
        chip_copy(i, mine).wait_send()
        return 0

    lax.fori_loop(0, 15, left_done, 0)

    def left_core(p, _):
        core_share(c, p).wait_send()
        piece_out(0, p).wait()
        piece_out(1, p).wait()
        return 0

    lax.fori_loop(0, 16, left_core, 0)
    each_kept(lambda copy: copy.wait_send())
    hid_out.wait()
    for copy in sent:
        copy.wait_send()


def hand_over(
    hid_in, pieces_in, bias_in, hid, g_self, g_neigh, g_bias,
    hid_held, pieces, grads, bias_held, sem_in, sem_out,
):
    def quarter(i):
        return pl.ds(4 * i, 4)

    halves = [pl.ds(512 * h, 512) for h in range(2)]
    inward = [
        pltpu.make_async_copy(pieces_in.at[:, quarter(i)], pieces.at[:, quarter(i)], sem_in.at[i])
        for i in range(4)
    ]
    inward += [
        pltpu.make_async_copy(hid_in.at[h], hid_held.at[h], sem_in.at[4 + k])
        for k, h in enumerate(halves)
    ]
    inward += [pltpu.make_async_copy(bias_in, bias_held, sem_in.at[6])]
    outward = [
        pltpu.make_async_copy(
            grads.at[pl.ds(96 * i, 96)],
            (g_self, g_neigh)[i // 2].at[pl.ds(96 * (i % 2), 96)],
            sem_out.at[i],
        )
        for i in range(4)
    ]
    outward += [
        pltpu.make_async_copy(hid_held.at[h], hid.at[h], sem_out.at[4 + k])
        for k, h in enumerate(halves)
    ]
    outward += [pltpu.make_async_copy(bias_held, g_bias, sem_out.at[6])]
    for copy in inward:
        copy.start()
    for i in (0, 1, 2, 3, 4, 5, 6):
        inward[i].wait()
        if i < 4:
            for p in range(4 * i, 4 * i + 4):
                for core in range(2):
                    value = pieces[core, p].astype(F32)
                    for q in range(4):
                        lane = q * 256 + core * 128
                        grads[24 * p : 24 * p + 24, lane : lane + 128] = value[
                            24 * q : 24 * q + 24
                        ]
        outward[i].start()
    for copy in outward:
        copy.wait()


def local(node_feats, seed_feats, w_self, w_neigh, bias, send_list, nbr_slot, cotangent):
    vmem = pl.BlockSpec(memory_space=pltpu.VMEM)
    anywhere = pl.BlockSpec(memory_space=pl.ANY)
    V, DMA = pltpu.VMEM, pltpu.SemaphoreType.DMA
    made = pl.pallas_call(
        kernel,
        out_shape=(
            jax.ShapeDtypeStruct((1024, 256), BF),
            jax.ShapeDtypeStruct((2, 16, 96, 128), BF),
            jax.ShapeDtypeStruct((1, 1024), F32),
        ),
        in_specs=[anywhere] * 8,
        out_specs=(anywhere, anywhere, vmem),
        scratch_shapes=[
            V((16, 192, 256), BF),
            V((32, 256), I32),
            V((25, 1024), I32),
            V((1, 1024), F32),
            V((1024, 256), BF),
            V((1024, 128), I32),
            V((128, 256), I32),
            V((32, 192, 256), BF),
            V((32, 192, 256), BF),
            V((32, 1024, 256), BF),
            V((192, 1024), F32),
            V((4, 192, 1024), BF),
            V((4, 192, 1024), BF),
            V((4, 192, 256), BF),
            V((4, 192, 256), BF),
            V((256, 1024), F32),
            V((256, 1024), F32),
            V((256, 1024), BF),
            V((1024, 256), BF),
            V((256, 1024), BF),
            V((2, 1536, 128), F32),
            V((1536, 128), F32),
            V((4, 384, 128), F32),
            V((2, 4, 2, 96, 128), F32),
            V((2, 2, 96, 128), F32),
            V((4, 4, 24, 128), F32),
            V((2, 16, 96, 128), BF),
            V((3, 8, 256), F32),
            V((9, 8, 256), F32),
            V((4, 8, 256), F32),
            DMA((4, 32)),
            DMA((4, 32)),
            DMA((10, 4)),
            DMA((10, 4)),
            DMA((10, 4)),
            DMA((10, 4)),
            DMA((16,)),
            DMA((16,)),
            DMA((16,)),
            DMA((16,)),
            DMA((23,)),
            DMA((33,)),
            DMA((4, 4)),
            DMA((4, 4)),
        ],
        compiler_params=pltpu.CompilerParams(
            collective_id=0, has_side_effects=True, vmem_limit_bytes=60 << 20
        ),
        name="sage_layer",
    )(
        node_feats.T,
        seed_feats,
        w_self,
        w_neigh,
        bias.reshape(1, 1024),
        send_list.reshape(32, 256),
        nbr_slot.T,
        cotangent,
    )
    hidden, grad_self, grad_neigh, grad_bias = pl.pallas_call(
        hand_over,
        out_shape=(
            jax.ShapeDtypeStruct((1024, 256), BF),
            jax.ShapeDtypeStruct((192, 1024), F32),
            jax.ShapeDtypeStruct((192, 1024), F32),
            jax.ShapeDtypeStruct((1, 1024), F32),
        ),
        in_specs=[anywhere] * 3,
        out_specs=(anywhere,) * 4,
        scratch_shapes=[
            V((1024, 256), BF),
            V((2, 16, 96, 128), BF),
            V((384, 1024), F32),
            V((1, 1024), F32),
            DMA((7,)),
            DMA((7,)),
        ],
        name="hand_over",
    )(*made)
    return hidden, grad_self, grad_neigh, grad_bias.reshape(1024)


def solution(mesh):
    placed = (
        P("seed", "feat"),
        P("feat", "seed"),
        P("feat", None),
        P("feat", None),
        P(),
        P("seed", None, None),
        P("seed", None),
        P("seed", "feat"),
    )
    return jax.shard_map(
        local,
        mesh=mesh,
        in_specs=placed,
        out_specs=(P("seed", "feat"), P("feat", None), P("feat", None), P()),
        check_vma=False,
    )
```
